128 devices in a mesh: dev: 128 (over y, x, z, core).
Axes of the slice: x: 4, y: 4, z: 4, core: 2. Of those that a mesh axis runs over, the one named last changes fastest.
Arguments:
- features: bfloat16 [32768, 128], P('dev'), may hold values from -6 to 6
- weight: bfloat16 [128, 256], replicated, may hold values from -0.5 to 0.5
- tile_values: bfloat16 [256, 32, 128, 128], P('dev'), may hold values from -0.09375 to 0.09375
- tile_cols: int32 [256, 32], P('dev'), may hold values from 0 to 255, as said below
- tile_counts: int32 [256, 32], P('dev'), may hold values from 0 to 16384, as said below
- cotangent: bfloat16 [32768, 256], P('dev'), may hold values from -6 to 6
Outputs:
- activations: bfloat16 [32768, 256], P('dev')
- features_grad: float32 [32768, 128], P('dev')
- weight_grad: float32 [128, 256], P('dev')
The draws below stay inside these ranges and needn't reach their ends.
Inputs may be any that keep to these rules, and one draw needn't show every extreme that they name: `tile_cols`: within a row block the column blocks of the slots are distinct. `tile_counts`: A slot is live where its count is above 0; the live slots of a row block come first, every row block has at least half of its 32 slots live (and at least one), and some row block has all live.
All inputs are finite; a program needn't handle non-finite values.
Results may differ from the reference program's by a relative error of at most 0.0061.
Values may be sent and summed in bfloat16 or wider, within the bound.
A program may use at most 128 MiB of HBM per device.

```python
import jax
import jax.numpy as jnp
from jax import lax

FIN = 128
HID = 256
TILE = 128
TILE_SLOTS = 32
NBLOCKS = 256
NVERT = 32768


def draw_tile_cols(key, part):
    key = jax.random.fold_in(key, 11)
    row_keys = jax.random.split(key, NBLOCKS)

    def one_row(row_key):
        return jax.random.permutation(row_key, NBLOCKS)[:TILE_SLOTS]
    return jax.vmap(one_row)(row_keys).astype(jnp.int32)


def draw_tile_counts(key, part):
    key = jax.random.fold_in(key, 23)
    key_live, key_full, key_edges = jax.random.split(key, 3)
    lowest = max(1, TILE_SLOTS // 2)
    live_count = jax.random.randint(key_live, (NBLOCKS,), lowest, TILE_SLOTS + 1)
    full_row = jax.random.randint(key_full, (), 0, NBLOCKS)
    row_index = jnp.arange(NBLOCKS)
    slot_index = jnp.arange(TILE_SLOTS)
    live_count = jnp.where(row_index == full_row, TILE_SLOTS, live_count)
    edges = jax.random.randint(key_edges, (NBLOCKS, TILE_SLOTS), 1, TILE * TILE + 1)
    corner = (row_index[:, None] == full_row) & (slot_index[None, :] == 0)
    edges = jnp.where(corner, TILE * TILE, edges)
    counts = jnp.where(slot_index[None, :] < live_count[:, None], edges, 0)
    return counts.astype(jnp.int32)


def block_levels(rng, dims, pieces, smallest, high):
    def one(position, shards_of):
        draws = jax.random.uniform(jax.random.fold_in(jax.random.fold_in(rng, 6), position), (shards_of,), jnp.float32, smallest / len(pieces), high / len(pieces))
        return jnp.repeat(jnp.exp(draws), dims[position] // shards_of).reshape((-1,) + (1,) * (len(dims) - position - 1))

    factor_of = one(*pieces[0])
    for cut in pieces[1:]:
        factor_of = factor_of * one(*cut)
    return factor_of


def centred(stream_key, dims, deviation, most, cuts=(), held_as=jnp.bfloat16):
    entries = jax.random.normal(stream_key, dims, jnp.float32) * deviation
    if len(cuts) > 0:
        entries = block_levels(stream_key, dims, cuts, -0.22, 0.18) * entries
    return jnp.clip(entries, min=-most, max=most).astype(held_as)


def setup_inputs(seed: int = 0) -> dict:
    arg_keys = jax.random.split(jax.random.key(seed), 7)
    return {
        "features": centred(arg_keys[0], (NVERT, FIN), 1.0, 6.0, ((0, 128),)),
        "weight": centred(arg_keys[1], (FIN, HID), FIN ** -0.5, 0.5),
        "tile_values": centred(arg_keys[2], (NBLOCKS, TILE_SLOTS, TILE, TILE), (TILE * TILE_SLOTS) ** -0.5, 0.09375, ((0, 128),)),
        "tile_cols": draw_tile_cols(jax.random.fold_in(arg_keys[6], 71), 0),
        "tile_counts": draw_tile_counts(jax.random.fold_in(arg_keys[6], 71), 0),
        "cotangent": centred(arg_keys[5], (NVERT, HID), 1.0, 6.0, ((0, 128),)),
    }


def reference(features, weight, tile_values, tile_cols, tile_counts, cotangent):
    block_count, slot_count, tile_size, _ = tile_values.shape
    in_width = features.shape[1]
    feature_blocks = features.reshape(block_count, tile_size, in_width)
    live = (tile_counts > 0).astype(jnp.float32)

    def forward_block(inputs):
        values, columns, alive = inputs
        picked = feature_blocks[columns].astype(jnp.float32)
        products = jnp.einsum("sij,sjf->sif", values.astype(jnp.float32), picked)
        return jnp.sum(products * alive[:, None, None], axis=0)

    summed = lax.map(forward_block, (tile_values, tile_cols, live))
    aggregated = summed.reshape(-1, in_width).astype(jnp.bfloat16)
    pre = jnp.dot(aggregated, weight, preferred_element_type=jnp.float32)
    activations = (jax.nn.silu(pre)).astype(jnp.bfloat16)
    sigma = jax.nn.sigmoid(pre)
    delta = (cotangent.astype(jnp.float32) * sigma * (1.0 + pre * (1.0 - sigma))).astype(jnp.bfloat16)
    back = jnp.dot(delta, weight.T, preferred_element_type=jnp.float32).astype(jnp.bfloat16)
    back_blocks = back.reshape(block_count, tile_size, in_width)

    def backward_step(total, inputs):
        values, columns, alive, vectors = inputs
        terms = jnp.einsum("sij,if->sjf", values.astype(jnp.float32), vectors.astype(jnp.float32))
        rounded = lax.optimization_barrier(terms.astype(jnp.bfloat16)).astype(jnp.float32)
        return total.at[columns].add(rounded * alive[:, None, None]), None

    start_total = jnp.zeros((block_count, tile_size, in_width), jnp.float32)
    total, _ = lax.scan(backward_step, start_total, (tile_values, tile_cols, live, back_blocks))
    features_grad = total.reshape(-1, in_width)
    weight_grad = jnp.dot(aggregated.T, delta, preferred_element_type=jnp.float32)
    return activations, features_grad, weight_grad
```

```python
import functools

import jax
import jax.numpy as jnp
import numpy as np
from jax import lax
from jax.experimental import pallas as pl
from jax.experimental.pallas import tpu as pltpu
from jax.sharding import PartitionSpec as P

MESH = pl.DeviceIdType.MESH
BF16, F32 = jnp.bfloat16, jnp.float32
SIDE = 4
TILE, SLOTS, FIN, HID = 128, 32, 128, 256
BLOCKS = 256
ROWS = (48, 48, 32)
STARTS = (0, 48, 96)
EXTRA = 16
CHUNK = (96, 96, 80)
ORDER = ((0, 1, 2), (1, 2, 0), (2, 0, 1))
HOPS = (1, 3, 2)


def column_table():
    table = np.zeros((3, 2, SIDE, SIDE, SIDE, 2), np.int32)
    for part in range(3):
        for place in np.ndindex(table.shape[1:]):
            core, half = place[0], place[4]
            at = {axis: place[1 + n] for n, axis in enumerate(ORDER[part])}
            device = ((at[0] * SIDE + at[1]) * SIDE + at[2]) * 2 + core
            table[(part,) + place] = device * 2 + half
    return table.reshape(3, BLOCKS)


def place_of_column(cols, part):
    core, half = (cols >> 1) & 1, cols & 1
    at = (cols >> 6, (cols >> 4) & 3, (cols >> 2) & 3)
    flat = core
    for axis in ORDER[part]:
        flat = flat * SIDE + at[axis]
    return flat * 2 + half


def kernel(
    place_ref, slot_ref, features_hbm, weight_hbm, tiles_hbm, cotangent_hbm,
    act_ref, grad_ref, weight_grad_ref,
    x_ref, w_ref, tiles, ct_ref,
    f0, f1, f2, t0, t1, t2, out0, out1, out2, in0, in1, in2, own0, own1, own2,
    pass_up0, pass_up1, pass_up2, pass_down0, pass_down1, pass_down2,
    end_up0, end_up1, end_up2, end_down0, end_down1, end_down2,
    b0, b1, b2, rb0, rb1, rb2, c0, c1, c2, rc0, rc1, rc2, wg_ref,
    load_sem, g1s, g1r, g2s, g2r, g3s, g3r, gcs, gcr,
    xs, xr, pas, par, pes, per, bs, br, cs, cr,
):
    parts = range(3)
    gathered = (f0, f1, f2)
    terms = (t0, t1, t2)
    to_twin, from_twin, own = (out0, out1, out2), (in0, in1, in2), (own0, own1, own2)
    pass_up, pass_down = (pass_up0, pass_up1, pass_up2), (pass_down0, pass_down1, pass_down2)
    end_up, end_down = (end_up0, end_up1, end_up2), (end_down0, end_down1, end_down2)
    mid, mid_in = (b0, b1, b2), (rb0, rb1, rb2)
    last, last_in = (c0, c1, c2), (rc0, rc1, rc2)

    me = lax.axis_index("dev")
    core = me % 2
    at = (me // 32, (me // 8) % 4, (me // 2) % 4)

    def device(axis, hop):
        moved = [(at[a] + hop) % SIDE if a == axis else at[a] for a in range(3)]
        return (((moved[0] * SIDE + moved[1]) * SIDE + moved[2]) * 2 + core,)

    twin = (me + 1 - 2 * core,)

    loads = [
        pltpu.make_async_copy(src, dst, load_sem.at[n])
        for n, (src, dst) in enumerate(
            ((features_hbm, x_ref), (weight_hbm, w_ref), (tiles_hbm, tiles), (cotangent_hbm, ct_ref))
        )
    ]
    for load in loads:
        load.start()

    barrier = pltpu.get_barrier_semaphore()
    for axis in range(3):
        for hop in HOPS:
            pl.semaphore_signal(barrier, inc=1, device_id=device(axis, hop), device_id_type=MESH)
    pl.semaphore_signal(barrier, inc=1, device_id=twin, device_id_type=MESH)

    for p in parts:
        gathered[p][2 * BLOCKS // 2] = jnp.zeros((ROWS[p], FIN), BF16)
        terms[p][2 * SLOTS] = jnp.zeros((ROWS[p], TILE), BF16)

    def flat(p, slow, middle, fast):
        return (slow * SIDE + middle) * SIDE + fast

    i3 = [at[ORDER[p][0]] for p in parts]
    i2 = [at[ORDER[p][1]] for p in parts]
    i1 = [at[ORDER[p][2]] for p in parts]
    loads[0].wait()
    for p in parts:
        place = (core * 64 + flat(p, i3[p], i2[p], i1[p])) * 2
        for half in range(2):
            gathered[p][place + half] = x_ref[pl.ds(half * TILE + STARTS[p], ROWS[p]), :]

    pl.semaphore_wait(barrier, 10)

    sends = []

    def send(src, dst, ssem, rsem, to):
        copy = pltpu.make_async_remote_copy(
            src_ref=src, dst_ref=dst, send_sem=ssem, recv_sem=rsem, device_id=to, device_id_type=MESH
        )
        copy.start()
        sends.append(copy)

    def arrived(dst, ssem, rsem):
        pltpu.make_async_remote_copy(
            src_ref=dst, dst_ref=dst, send_sem=ssem, recv_sem=rsem, device_id=twin, device_id_type=MESH
        ).wait_recv()

    def chunk(p, slow, middle, fast, count=1):
        return gathered[p].at[pl.ds((core * 64 + flat(p, slow, middle, fast)) * 2, 2 * count)]

    for p in parts:
        mine = chunk(p, i3[p], i2[p], i1[p])
        for n, hop in enumerate(HOPS):
            send(mine, mine, g1s.at[p, n], g1r.at[p, n], device(ORDER[p][2], hop))
    for r in range(4):
        for p in parts:
            fast = i1[p] if r == 0 else (i1[p] + SIDE - HOPS[r - 1]) % SIDE
            ref = chunk(p, i3[p], i2[p], fast)
            if r > 0:
                arrived(ref, g1s.at[p, r - 1], g1r.at[p, r - 1])
            for n, hop in enumerate(HOPS):
                send(ref, ref, g2s.at[p, r * 3 + n], g2r.at[p, r * 3 + n], device(ORDER[p][1], hop))

    def slab(p, slow, r):
        middle = i2[p] if r == 0 else (i2[p] + SIDE - HOPS[r - 1]) % SIDE
        return chunk(p, slow, middle, 0, SIDE)

    def to_the_twin(p, ref, n):
        send(ref, ref, gcs.at[p, n], gcr.at[p], twin)

    def pass_on(p, r):
        up = slab(p, (i3[p] + 3) % SIDE, r)
        down = slab(p, (i3[p] + 1) % SIDE, r)
        arrived(up, g3s.at[p, 2 * r], g3r.at[p, 2 * r])
        if r < 2:
            send(up, up, g3s.at[p, 8 + r], g3r.at[p, 8 + r], device(ORDER[p][0], 1))
        to_the_twin(p, up, 4 + 2 * r)
        arrived(down, g3s.at[p, 2 * r + 1], g3r.at[p, 2 * r + 1])
        if r >= 2:
            send(down, down, g3s.at[p, 8 + r], g3r.at[p, 8 + r], device(ORDER[p][0], 3))
        to_the_twin(p, down, 5 + 2 * r)

    for r in range(4):
        for p in parts:
            ref = slab(p, i3[p], r)
            if r > 0:
                middle = (i2[p] + SIDE - HOPS[r - 1]) % SIDE
                for s in range(4):
                    fast = i1[p] if s == 0 else (i1[p] + SIDE - HOPS[s - 1]) % SIDE
                    n = s * 3 + r - 1
                    arrived(chunk(p, i3[p], middle, fast), g2s.at[p, n], g2r.at[p, n])
            send(ref, ref, g3s.at[p, 2 * r], g3r.at[p, 2 * r], device(ORDER[p][0], 1))
            send(ref, ref, g3s.at[p, 2 * r + 1], g3r.at[p, 2 * r + 1], device(ORDER[p][0], 3))
            to_the_twin(p, ref, r)
        if r > 0:
            for p in parts:
                pass_on(p, r - 1)
    for p in parts:
        pass_on(p, 3)
    for r in range(4):
        for p in parts:
            ref = slab(p, (i3[p] + 2) % SIDE, r)
            arrived(ref, g3s.at[p, 8 + r], g3r.at[p, 8 + r])
            to_the_twin(p, ref, 12 + r)
    for load in loads[1:]:
        load.wait()
    for p in parts:
        arrived(gathered[p].at[pl.ds((1 - core) * 128, 128)], gcs.at[p, 0], gcr.at[p])

    def block_of(slot):
        return jnp.concatenate([gathered[p][place_ref[p, slot]] for p in parts], axis=0)

    def forward_step(n, totals):
        new = []
        for b in range(2):
            total = totals[b]
            for k in range(2):
                slot = n * 4 + k * 2
                left = jnp.concatenate([tiles[b, slot], tiles[b, slot + 1]], axis=1)
                right = jnp.concatenate([block_of(b * SLOTS + slot), block_of(b * SLOTS + slot + 1)], axis=0)
                total = total + jnp.dot(left, right, preferred_element_type=F32)
            new.append(total)
        return tuple(new)

    zero = jnp.zeros((TILE, FIN), F32)
    totals = lax.fori_loop(0, SLOTS // 4, forward_step, (zero, zero))
    aggregated = jnp.concatenate(totals, axis=0).astype(BF16)
    weight = w_ref[...]
    pre = jnp.dot(aggregated, weight, preferred_element_type=F32)
    sigma = jax.nn.sigmoid(pre)
    act_ref[...] = (pre * sigma).astype(BF16)
    delta = (ct_ref[...].astype(F32) * sigma * (1.0 + pre * (1.0 - sigma))).astype(BF16)
    back = lax.dot_general(
        weight, delta, (((1,), (1,)), ((), ())), preferred_element_type=F32
    ).astype(BF16)
    weight_terms = lax.dot_general(
        aggregated, delta, (((0,), (0,)), ((), ())), preferred_element_type=F32
    )
    for half in range(2):
        wg_ref[pl.ds(half * FIN, FIN), :] = weight_terms[:, half * TILE : (half + 1) * TILE]

    for b in range(2):
        left = back[:, b * TILE : (b + 1) * TILE]

        def term_step(n, carry, b=b, left=left):
            for k in range(2):
                slot = n * 4 + k * 2
                right = jnp.concatenate([tiles[b, slot], tiles[b, slot + 1]], axis=1)
                both = jnp.dot(left, right, preferred_element_type=F32).astype(BF16)
                for half in range(2):
                    for p in parts:
                        terms[p][b * SLOTS + slot + half] = both[
                            STARTS[p] : STARTS[p] + ROWS[p], half * TILE : (half + 1) * TILE
                        ]
            return carry

        lax.fori_loop(0, SLOTS // 4, term_step, 0)

    row = lax.broadcasted_iota(jnp.int32, (EXTRA, TILE), 0)

    def weight_rows(p, which, position):
        slow, middle, fast = position // 16, (position // 4) % 4, position % 4
        moved = {ORDER[p][0]: slow, ORDER[p][1]: middle, ORDER[p][2]: fast}
        target = ((moved[0] * SIDE + moved[1]) * SIDE + moved[2]) * 2 + which
        first = wg_ref[pl.ds(target, 1), :]
        second = wg_ref[pl.ds(FIN + target, 1), :]
        return jnp.where(row == 0, first, jnp.where(row == 1, second, 0.0)).astype(BF16)

    def spread(p, which, slow, dst, extra):
        def step(n, carry):
            values = []
            for k in range(2):
                position = slow * 16 + n * 2 + k
                halves = []
                for half in range(2):
                    entry = (which * 64 + position) * 2 + half
                    halves.append(terms[p][slot_ref[p, 0, entry]] + terms[p][slot_ref[p, 1, entry]])
                if p == 2:
                    halves.append(weight_rows(p, which, position))
                value = jnp.concatenate(halves, axis=0)
                if extra is not None:
                    value = value + extra[position]
                values.append((position, value))
            for position, value in values:
                dst[position] = value
            return carry

        lax.fori_loop(0, 8, step, 0)

    away = (2, 1, 3, 0)
    for n, o in enumerate(away):
        for p in parts:
            slow = (i3[p] + o) % SIDE
            spread(p, 1 - core, slow, to_twin[p], None)
            send(
                to_twin[p].at[pl.ds(slow * 16, 16)], from_twin[p].at[pl.ds(slow * 16, 16)],
                xs.at[p, n], xr.at[p, n], twin,
            )

    def part_of(ref, slow, middle):
        return ref.at[pl.ds(slow * 16 + middle * 4, 4)]

    def slab_at(p, q):
        return (i2[p] + away[q]) % SIDE

    for n, o in enumerate(away):
        for p in parts:
            slow = (i3[p] + o) % SIDE
            ref = from_twin[p].at[pl.ds(slow * 16, 16)]
            arrived(ref, xs.at[p, n], xr.at[p, n])
            spread(p, core, slow, own[p], from_twin[p])
            up, down = device(ORDER[p][0], 1), device(ORDER[p][0], 3)
            if o == 2:
                for q in range(2):
                    send(part_of(own[p], slow, slab_at(p, q)), pass_up[p].at[q], pas.at[p, q], par.at[p, q], up)
                    send(
                        part_of(own[p], slow, slab_at(p, q + 2)), pass_down[p].at[q],
                        pas.at[p, 2 + q], par.at[p, 2 + q], down,
                    )
            if o == 1:
                for q in range(2, 4):
                    send(part_of(own[p], slow, slab_at(p, q)), end_up[p].at[q], pes.at[p, q], per.at[p, q], up)
            if o == 3:
                for q in range(2):
                    send(
                        part_of(own[p], slow, slab_at(p, q)), end_down[p].at[q],
                        pes.at[p, 4 + q], per.at[p, 4 + q], down,
                    )
    for q in range(2):
        for p in parts:
            up, down = device(ORDER[p][0], 1), device(ORDER[p][0], 3)
            arrived(pass_up[p].at[q], pas.at[p, q], par.at[p, q])
            ref = part_of(own[p], (i3[p] + 1) % SIDE, slab_at(p, q))
            ref[...] = ref[...] + pass_up[p][q]
            send(ref, end_up[p].at[q], pes.at[p, q], per.at[p, q], up)
            arrived(pass_down[p].at[q], pas.at[p, 2 + q], par.at[p, 2 + q])
            ref = part_of(own[p], (i3[p] + 3) % SIDE, slab_at(p, q + 2))
            ref[...] = ref[...] + pass_down[p][q]
            send(ref, end_down[p].at[q + 2], pes.at[p, 6 + q], per.at[p, 6 + q], down)
    for q in range(4):
        for p in parts:
            arrived(end_up[p].at[q], pes.at[p, q], per.at[p, q])
            arrived(end_down[p].at[q], pes.at[p, 4 + q], per.at[p, 4 + q])
            ref = part_of(own[p], i3[p], slab_at(p, q))
            total = ref[...].astype(F32) + end_up[p][q].astype(F32) + end_down[p][q].astype(F32)
            mid[p][q] = total.astype(BF16)
            if q < 3:
                send(mid[p].at[q], mid_in[p].at[q], bs.at[p, q], br.at[p, q], device(ORDER[p][1], away[q]))
    for p in parts:
        for q in range(3):
            arrived(mid_in[p].at[q], bs.at[p, q], br.at[p, q])
        total = mid[p][3].astype(F32)
        for q in range(3):
            total = total + mid_in[p][q].astype(F32)
        last[p][...] = total.astype(BF16)
        for q in range(3):
            place = (i1[p] + away[q]) % SIDE
            send(last[p].at[place], last_in[p].at[q], cs.at[p, q], cr.at[p, q], device(ORDER[p][2], away[q]))
    results = []
    for p in parts:
        for q in range(3):
            arrived(last_in[p].at[q], cs.at[p, q], cr.at[p, q])
        total = last[p][i1[p]].astype(F32)
        for q in range(3):
            total = total + last_in[p][q].astype(F32)
        results.append(total)
    for half in range(2):
        block = jnp.concatenate(
            [results[p][half * ROWS[p] : (half + 1) * ROWS[p]] for p in parts], axis=0
        )
        grad_ref[pl.ds(half * TILE, TILE), :] = block.T
    weight_grad_ref[:, pl.ds(0, TILE)] = results[2][64:65]
    weight_grad_ref[:, pl.ds(TILE, TILE)] = results[2][65:66]
    for copy in sends:
        copy.wait_send()


def on_device(features, weight, tile_values, tile_cols, tile_counts, cotangent):
    live = tile_counts > 0
    cols = tile_cols.reshape(-1)
    place = jnp.stack(
        [jnp.where(live.reshape(-1), place_of_column(cols, p), BLOCKS) for p in range(3)]
    )
    table = jnp.asarray(column_table())
    slot = jnp.arange(2 * SLOTS, dtype=jnp.int32).reshape(2, SLOTS)
    hit = (table[:, None, :, None] == tile_cols[None, :, None, :]) & live[None, :, None, :]
    slots = 2 * SLOTS + jnp.sum(jnp.where(hit, slot[None, :, None, :] - 2 * SLOTS, 0), axis=3)

    def vmem(*shape, dtype=BF16):
        return pltpu.VMEM(shape, dtype)

    def three(*lead, rows, lanes=128):
        return [vmem(*lead, rows[p], lanes) for p in range(3)]

    dma = pltpu.SemaphoreType.DMA
    smem, anywhere, in_vmem = (
        pl.BlockSpec(memory_space=pltpu.SMEM),
        pl.BlockSpec(memory_space=pl.ANY),
        pl.BlockSpec(memory_space=pltpu.VMEM),
    )
    scratch = (
        [vmem(256, FIN), vmem(FIN, HID), vmem(2, SLOTS, TILE, TILE), vmem(256, HID)]
        + three(BLOCKS + 1, rows=ROWS)
        + three(2 * SLOTS + 1, rows=ROWS)
        + three(64, rows=CHUNK)
        + three(64, rows=CHUNK)
        + three(64, rows=CHUNK)
        + three(2, 4, rows=CHUNK)
        + three(2, 4, rows=CHUNK)
        + three(4, 4, rows=CHUNK)
        + three(4, 4, rows=CHUNK)
        + three(4, 4, rows=CHUNK)
        + three(3, 4, rows=CHUNK)
        + three(4, rows=CHUNK)
        + three(3, rows=CHUNK)
        + [vmem(2 * FIN, TILE, dtype=F32)]
        + [dma((4,))]
        + [dma((3, 3)), dma((3, 3)), dma((3, 12)), dma((3, 12)), dma((3, 12)), dma((3, 12)), dma((3, 16)), dma((3,))]
        + [dma((3, 4)), dma((3, 4)), dma((3, 4)), dma((3, 4)), dma((3, 8)), dma((3, 8))]
        + [dma((3, 3)), dma((3, 3)), dma((3, 3)), dma((3, 3))]
    )
    return pl.pallas_call(
        kernel,
        out_shape=(
            jax.ShapeDtypeStruct((256, HID), BF16),
            jax.ShapeDtypeStruct((256, FIN), F32),
            jax.ShapeDtypeStruct((1, HID), F32),
        ),
        in_specs=[smem, smem, anywhere, anywhere, anywhere, anywhere],
        out_specs=(in_vmem, in_vmem, in_vmem),
        scratch_shapes=scratch,
        compiler_params=pltpu.CompilerParams(
            collective_id=0, has_side_effects=True, vmem_limit_bytes=56 << 20
        ),
        name="graph_layer",
    )(place, slots, features, weight, tile_values, cotangent)


def solution(mesh):
    return jax.shard_map(
        on_device,
        mesh=mesh,
        in_specs=(
            P("dev", None),
            P(),
            P("dev", None, None, None),
            P("dev", None),
            P("dev", None),
            P("dev", None),
        ),
        out_specs=(P("dev", None), P("dev", None), P("dev", None)),
        check_vma=False,
    )
```

```python
import jax
import jax.numpy as jnp
from jax import lax
from jax.experimental import pallas as pl
from jax.experimental.pallas import tpu as pltpu
from jax.sharding import PartitionSpec as P

MESH = pl.DeviceIdType.MESH
BF16, F32, I32 = jnp.bfloat16, jnp.float32, jnp.int32
SIDE = 4
TILE, SLOTS, FIN, HID = 128, 32, 128, 256
CHUNKS = 64
UNIT = 16
UNITS = (6, 5, 5)
BASE = (0, 129 * 6, 129 * 11)
ROWS = (48, 48, 32)
STARTS = (0, 48, 96)
EXTRA = 16
CHUNK = (96, 96, 80)
NONE = 4 * SLOTS
ORDER = ((0, 1, 2), (1, 2, 0), (2, 0, 1))
HOPS = (1, 3, 2)


def pick(which, values):
    return jnp.where(which == 0, values[0], jnp.where(which == 1, values[1], values[2]))


def kernel(
    features_hbm, weight_hbm, tiles_hbm, cols_hbm, counts_hbm, cotangent_hbm,
    act_hbm, grad_ref, weight_grad_ref,
    gathered, w_ref, tiles, ct_ref, cols_ref, counts_ref, cols_smem, counts_smem, act_ref,
    place_ref, place_smem, slot_ref, twin_slot_out, twin_slot_ref, slot_smem, t0, t1, t2, own0, own1, own2,
    pass_up0, pass_up1, pass_up2, pass_down0, pass_down1, pass_down2,
    end_up0, end_up1, end_up2, end_down0, end_down1, end_down2,
    b0, b1, b2, rb0, rb1, rb2, c0, c1, c2, rc0, rc1, rc2, wg_ref, twin_wg_ref,
    load_sem, act_sem, table_sem, g1s, g1r, g2s, g2r, gos, gor, g3s, g3r, gcs, gcr, ts, tr, es, er,
    pas, par, pes, per, bs, br, cs, cr,
):
    parts = range(3)
    terms, own = (t0, t1, t2), (own0, own1, own2)
    pass_up, pass_down = (pass_up0, pass_up1, pass_up2), (pass_down0, pass_down1, pass_down2)
    end_up, end_down = (end_up0, end_up1, end_up2), (end_down0, end_down1, end_down2)
    mid, mid_in = (b0, b1, b2), (rb0, rb1, rb2)
    last, last_in = (c0, c1, c2), (rc0, rc1, rc2)

    me = lax.axis_index("dev")
    core = me % 2
    at = (me // 32, (me // 8) % 4, (me // 2) % 4)
    strides = (32, 8, 2)

    def device(axis, hop):
        return (me + ((at[axis] + hop) % SIDE - at[axis]) * strides[axis],)

    twin = (me + 1 - 2 * core,)

    barrier = pltpu.get_barrier_semaphore()
    for hop in (2, 1, 3):
        for axis in range(3):
            pl.semaphore_signal(barrier, inc=1, device_id=device(axis, hop), device_id_type=MESH)
    pl.semaphore_signal(barrier, inc=1, device_id=twin, device_id_type=MESH)

    turn = [(core + p) % 3 for p in parts]
    i3, i2, i1 = ([pick((turn[p] + n) % 3, at) for p in parts] for n in range(3))
    s3, s2, s1 = ([pick((turn[p] + n) % 3, strides) for p in parts] for n in range(3))

    def move(index, stride, hop):
        return (me + ((index + hop) % SIDE - index) * stride,)

    def chunk(p, slow, middle, fast, count=1):
        at_chunk = core * CHUNKS + (slow * SIDE + middle) * SIDE + fast
        return gathered.at[pl.ds(BASE[p] + at_chunk * UNITS[p], count * UNITS[p])]

    loads = []

    def load(src, dst):
        copy = pltpu.make_async_copy(src, dst, load_sem.at[len(loads)])
        copy.start()
        loads.append(copy)

    for p, first, unit, count in ((0, 0, 0, 3), (1, 3, 0, 3), (2, 6, 0, 2), (0, 8, 3, 3), (1, 11, 3, 2), (2, 13, 2, 3)):
        place = BASE[p] + (core * CHUNKS + (i3[p] * SIDE + i2[p]) * SIDE + i1[p]) * UNITS[p] + unit
        load(features_hbm.at[pl.ds(first, count)], gathered.at[pl.ds(place, count)])
    load(cols_hbm, cols_smem)
    load(counts_hbm, counts_smem)
    load(cols_hbm, cols_ref)
    load(counts_hbm, counts_ref)
    load(tiles_hbm, tiles)
    load(weight_hbm, w_ref)
    load(cotangent_hbm, ct_ref)

    sends = []

    def send(src, dst, ssem, rsem, to):
        copy = pltpu.make_async_remote_copy(
            src_ref=src, dst_ref=dst, send_sem=ssem, recv_sem=rsem, device_id=to, device_id_type=MESH
        )
        copy.start()
        sends.append(copy)

    def arrived(dst, ssem, rsem):
        pltpu.make_async_remote_copy(
            src_ref=dst, dst_ref=dst, send_sem=ssem, recv_sem=rsem, device_id=twin, device_id_type=MESH
        ).wait_recv()

    for copy in loads[:6]:
        copy.wait()
    pl.semaphore_wait(barrier, 10)

    def first_sends(p, r):
        fast = i1[p] if r == 0 else (i1[p] + SIDE - HOPS[r - 1]) % SIDE
        ref = chunk(p, i3[p], i2[p], fast)
        if r > 0:
            arrived(ref, g1s.at[p, r - 1], g1r.at[p, r - 1])
        for n, hop in enumerate(HOPS):
            send(ref, ref, g2s.at[p, r * 3 + n], g2r.at[p, r * 3 + n], move(i2[p], s2[p], hop))
        return ref

    for p in parts:
        mine = chunk(p, i3[p], i2[p], i1[p])
        for n, hop in enumerate(HOPS):
            send(mine, mine, g1s.at[p, n], g1r.at[p, n], move(i1[p], s1[p], hop))
    for r in range(4):
        refs = [first_sends(p, r) for p in parts]
        for p in parts:
            for n, hop in enumerate((1, 3)):
                k = r * 2 + n
                send(refs[p], refs[p], gos.at[p, k], gor.at[p, k], move(i3[p], s3[p], hop))

    def slab(p, slow, r):
        middle = i2[p] if r == 0 else (i2[p] + SIDE - HOPS[r - 1]) % SIDE
        return chunk(p, slow, middle, 0, SIDE)

    def to_the_twin(p, ref, n):
        send(ref, ref, gcs.at[p, n], gcr.at[p], twin)

    def slab_arrived(p, r, slow, n):
        ref = slab(p, slow, r)
        if r == 0:
            for s in range(4):
                fast = i1[p] if s == 0 else (i1[p] + SIDE - HOPS[s - 1]) % SIDE
                arrived(chunk(p, slow, i2[p], fast), gos.at[p, s * 2 + n], gor.at[p, s * 2 + n])
        else:
            arrived(ref, g3s.at[p, 2 * r + n], g3r.at[p, 2 * r + n])
        return ref

    def pass_on(p, r):
        up = slab_arrived(p, r, (i3[p] + 3) % SIDE, 0)
        if r < 2:
            send(up, up, g3s.at[p, 8 + r], g3r.at[p, 8 + r], move(i3[p], s3[p], 1))
        to_the_twin(p, up, 4 + 2 * r)
        down = slab_arrived(p, r, (i3[p] + 1) % SIDE, 1)
        if r >= 2:
            send(down, down, g3s.at[p, 8 + r], g3r.at[p, 8 + r], move(i3[p], s3[p], 3))
        to_the_twin(p, down, 5 + 2 * r)

    for p in parts:
        to_the_twin(p, slab(p, i3[p], 0), 0)

    for p in parts:
        gathered[pl.ds(BASE[p] + 2 * CHUNKS * UNITS[p], UNITS[p])] = jnp.zeros((UNITS[p], UNIT, FIN), BF16)
        terms[p][NONE] = jnp.zeros((ROWS[p], TILE), BF16)
    for copy in loads[6:]:
        copy.wait()
    cols = cols_ref[...]
    live = counts_ref[...] > 0
    where = (cols >> 6, (cols >> 4) & 3, (cols >> 2) & 3)
    col_core, half = (cols >> 1) & 1, jnp.where(live, cols & 1, 0)
    starts = []
    for p in parts:
        turned = (col_core + p) % 3
        flat = col_core
        for n in range(3):
            flat = flat * SIDE + pick((turned + n) % 3, where)
        starts.append(BASE[p] + jnp.where(live, flat, 2 * CHUNKS) * UNITS[p])
    place_ref[0] = starts[0] + 3 * half
    place_ref[1] = starts[1] + 3 * half
    place_ref[2] = jnp.where(half == 0, starts[1], starts[2]) + 2
    place_ref[3] = starts[2] + 3 * half
    place_copy = pltpu.make_async_copy(place_ref, place_smem, table_sem.at[0])
    place_copy.start()
    line = lax.broadcasted_iota(I32, (8, TILE), 0)
    lane = lax.broadcasted_iota(I32, (8, TILE), 1)
    digits = (lane >> 5, (lane >> 3) & 3, (lane >> 1) & 3)
    column = 0
    for axis in range(3):
        digit = pick(line & 3, [digits[ORDER[p].index(axis)] for p in parts])
        column = column * SIDE + digit
    column = column * 4 + (line >> 2) * 2 + (lane & 1)
    for b in range(2):
        def find(s, found, b=b):
            wanted = jnp.where(counts_smem[b, s] > 0, cols_smem[b, s], -1)
            return jnp.where(column == wanted, b * SLOTS + s, found)

        found = lax.fori_loop(0, SLOTS, find, jnp.full((8, TILE), NONE, I32))
        slot_ref[b] = found
        twin_slot_out[b] = jnp.where(found < NONE, found + 2 * SLOTS, NONE)
    send(twin_slot_out, twin_slot_ref, es.at[0], er.at[0], twin)
    slot_copy = pltpu.make_async_copy(slot_ref, slot_smem.at[pl.ds(0, 2)], table_sem.at[1])
    slot_copy.start()

    for r in range(1, 4):
        for p in parts:
            ref = slab(p, i3[p], r)
            middle = (i2[p] + SIDE - HOPS[r - 1]) % SIDE
            for s in range(4):
                fast = i1[p] if s == 0 else (i1[p] + SIDE - HOPS[s - 1]) % SIDE
                n = s * 3 + r - 1
                arrived(chunk(p, i3[p], middle, fast), g2s.at[p, n], g2r.at[p, n])
            send(ref, ref, g3s.at[p, 2 * r], g3r.at[p, 2 * r], move(i3[p], s3[p], 1))
            send(ref, ref, g3s.at[p, 2 * r + 1], g3r.at[p, 2 * r + 1], move(i3[p], s3[p], 3))
            to_the_twin(p, ref, r)
        for p in parts:
            pass_on(p, r - 1)
    for p in parts:
        pass_on(p, 3)
    for r in range(4):
        for p in parts:
            ref = slab(p, (i3[p] + 2) % SIDE, r)
            arrived(ref, g3s.at[p, 8 + r], g3r.at[p, 8 + r])
            to_the_twin(p, ref, 12 + r)
    place_copy.wait()
    slot_copy.wait()
    arrived(twin_slot_ref, es.at[0], er.at[0])
    twin_slot_copy = pltpu.make_async_copy(twin_slot_ref, slot_smem.at[pl.ds(2, 2)], table_sem.at[2])
    twin_slot_copy.start()
    for p in parts:
        arrived(
            gathered.at[pl.ds(BASE[p] + (1 - core) * CHUNKS * UNITS[p], CHUNKS * UNITS[p])], gcs.at[p, 0], gcr.at[p]
        )

    def block_of(b, slot):
        pieces = [
            gathered[pl.ds(place_smem[0, b, slot], 3)].reshape(3 * UNIT, FIN),
            gathered[pl.ds(place_smem[1, b, slot], 2)].reshape(2 * UNIT, FIN),
            gathered[place_smem[2, b, slot]],
            gathered[pl.ds(place_smem[3, b, slot], 2)].reshape(2 * UNIT, FIN),
        ]
        return jnp.concatenate(pieces, axis=0)

    def forward_step(n, totals):
        new = []
        for b in range(2):
            total = totals[b]
            for k in range(FORWARD_UNROLL):
                slot = (n * FORWARD_UNROLL + k) * 2
                left = jnp.concatenate([tiles[b, slot], tiles[b, slot + 1]], axis=1)
                right = jnp.concatenate([block_of(b, slot), block_of(b, slot + 1)], axis=0)
                total = total + jnp.dot(left, right, preferred_element_type=F32)
            new.append(total)
        return tuple(new)

    zero = jnp.zeros((TILE, FIN), F32)
    totals = lax.fori_loop(0, SLOTS // (2 * FORWARD_UNROLL), forward_step, (zero, zero))
    aggregated = jnp.concatenate(totals, axis=0).astype(BF16)
    weight = w_ref[...]
    pre = jnp.dot(aggregated, weight, preferred_element_type=F32)
    sigma = jax.nn.sigmoid(pre)
    act_ref[...] = (pre * sigma).astype(BF16)
    act_copy = pltpu.make_async_copy(act_ref, act_hbm, act_sem)
    act_copy.start()
    delta = (ct_ref[...].astype(F32) * sigma * (1.0 + pre * (1.0 - sigma))).astype(BF16)
    back = lax.dot_general(
        weight, delta, (((1,), (1,)), ((), ())), preferred_element_type=F32
    ).astype(BF16)

    for b in range(2):
        left_factor = back[:, b * TILE : (b + 1) * TILE]
        for group in range(2):
            def term_step(n, carry, b=b, group=group, left_factor=left_factor):
                for k in range(TERM_UNROLL):
                    slot = group * 16 + (n * TERM_UNROLL + k) * 2
                    right = jnp.concatenate([tiles[b, slot], tiles[b, slot + 1]], axis=1)
                    both = jnp.dot(left_factor, right, preferred_element_type=F32).astype(BF16)
                    for which in range(2):
                        for p in parts:
                            terms[p][b * SLOTS + slot + which] = both[
                                STARTS[p] : STARTS[p] + ROWS[p], which * TILE : (which + 1) * TILE
                            ]
                return carry

            lax.fori_loop(0, 8 // TERM_UNROLL, term_step, 0)
            for p in parts:
                first = b * SLOTS + group * 16
                n = b * 2 + group
                send(
                    terms[p].at[pl.ds(first, 16)], terms[p].at[pl.ds(2 * SLOTS + first, 16)],
                    ts.at[p, n], tr.at[p, n], twin,
                )
    weight_terms = lax.dot_general(
        aggregated, delta, (((0,), (0,)), ((), ())), preferred_element_type=F32
    )
    for which in range(2):
        wg_ref[pl.ds(which * FIN, FIN), :] = weight_terms[:, which * TILE : (which + 1) * TILE]
    send(wg_ref, twin_wg_ref, es.at[1], er.at[1], twin)
    twin_slot_copy.wait()
    for p in parts:
        for n in range(4):
            arrived(terms[p].at[pl.ds(2 * SLOTS + n * 16, 16)], ts.at[p, n], tr.at[p, n])
    arrived(twin_wg_ref, es.at[1], er.at[1])

    row = lax.broadcasted_iota(I32, (EXTRA, TILE), 0)

    def weight_rows(p, slow, middle, fast):
        moved = {ORDER[p][0]: slow, ORDER[p][1]: middle, ORDER[p][2]: fast}
        target = ((moved[0] * SIDE + moved[1]) * SIDE + moved[2]) * 2 + core
        rows = []
        for which in range(2):
            place = pl.ds(which * FIN + target, 1)
            rows.append(wg_ref[place, :] + twin_wg_ref[place, :])
        return jnp.where(row == 0, rows[0], jnp.where(row == 1, rows[1], 0.0)).astype(BF16)

    def spread(p, slow, middle, dst, extras):
        values = []
        for fast in range(SIDE):
            halves = []
            for which in range(2):
                entry = ((slow * SIDE + middle) * SIDE + fast) * 2 + which
                found = [terms[p][slot_smem[k, core * 4 + p, entry]] for k in range(4)]
                halves.append((found[0] + found[1]) + (found[2] + found[3]))
            if p == 2:
                halves.append(weight_rows(p, slow, middle, fast))
            value = jnp.concatenate(halves, axis=0)
            if extras:
                value = value.astype(F32)
                for extra in extras:
                    value = value + extra[fast].astype(F32)
                value = value.astype(BF16)
            values.append(value)
        for fast in range(SIDE):
            dst[fast] = values[fast]

    away = (2, 1, 3, 0)

    def middle_at(p, q):
        return (at[ORDER[p][1]] + away[q]) % SIDE

    def own_slab(p, o, q, extras=()):
        slow, middle = (at[ORDER[p][0]] + o) % SIDE, middle_at(p, q)
        ref = own[p].at[pl.ds((slow * SIDE + middle) * SIDE, SIDE)]
        spread(p, slow, middle, ref, extras)
        return ref

    up = [device(ORDER[p][0], 1) for p in parts]
    down = [device(ORDER[p][0], 3) for p in parts]
    for q in (0, 2, 1, 3):
        for p in parts:
            ref = own_slab(p, 2, q)
            if q < 2:
                send(ref, pass_up[p].at[q], pas.at[p, q], par.at[p, q], up[p])
            else:
                send(ref, pass_down[p].at[q - 2], pas.at[p, q], par.at[p, q], down[p])
    for q in range(2):
        for p in parts:
            send(own_slab(p, 1, q + 2), end_up[p].at[q + 2], pes.at[p, q + 2], per.at[p, q + 2], up[p])
            send(own_slab(p, 3, q), end_down[p].at[q], pes.at[p, 4 + q], per.at[p, 4 + q], down[p])
    for q in range(2):
        for p in parts:
            arrived(pass_up[p].at[q], pas.at[p, q], par.at[p, q])
            ref = own_slab(p, 1, q, (pass_up[p].at[q],))
            send(ref, end_up[p].at[q], pes.at[p, q], per.at[p, q], up[p])
            arrived(pass_down[p].at[q], pas.at[p, 2 + q], par.at[p, 2 + q])
            ref = own_slab(p, 3, q + 2, (pass_down[p].at[q],))
            send(ref, end_down[p].at[q + 2], pes.at[p, 6 + q], per.at[p, 6 + q], down[p])
    for q in range(4):
        for p in parts:
            arrived(end_up[p].at[q], pes.at[p, q], per.at[p, q])
            arrived(end_down[p].at[q], pes.at[p, 4 + q], per.at[p, 4 + q])
            spread(
                p, at[ORDER[p][0]], middle_at(p, q), mid[p].at[q], (end_up[p].at[q], end_down[p].at[q])
            )
            if q < 3:
                send(mid[p].at[q], mid_in[p].at[q], bs.at[p, q], br.at[p, q], device(ORDER[p][1], away[q]))
    for p in parts:
        for q in range(3):
            arrived(mid_in[p].at[q], bs.at[p, q], br.at[p, q])
        total = mid[p][3].astype(F32)
        for q in range(3):
            total = total + mid_in[p][q].astype(F32)
        last[p][...] = total.astype(BF16)
        for q in range(3):
            place = (at[ORDER[p][2]] + away[q]) % SIDE
            send(last[p].at[place], last_in[p].at[q], cs.at[p, q], cr.at[p, q], device(ORDER[p][2], away[q]))
    results = []
    for p in parts:
        for q in range(3):
            arrived(last_in[p].at[q], cs.at[p, q], cr.at[p, q])
        total = last[p][at[ORDER[p][2]]].astype(F32)
        for q in range(3):
            total = total + last_in[p][q].astype(F32)
        results.append(total)
    for which in range(2):
        block = jnp.concatenate(
            [results[p][which * ROWS[p] : (which + 1) * ROWS[p]] for p in parts], axis=0
        )
        grad_ref[pl.ds(which * TILE, TILE), :] = block.T
    weight_grad_ref[:, pl.ds(0, TILE)] = results[2][64:65]
    weight_grad_ref[:, pl.ds(TILE, TILE)] = results[2][65:66]
    act_copy.wait()
    for copy in sends:
        copy.wait_send()


FORWARD_UNROLL = 4
TERM_UNROLL = 4


def on_device(features, weight, tile_values, tile_cols, tile_counts, cotangent):
    def vmem(*shape, dtype=BF16):
        return pltpu.VMEM(shape, dtype)

    def three(*lead, rows):
        return [vmem(*lead, rows[p], TILE) for p in range(3)]

    dma = pltpu.SemaphoreType.DMA
    anywhere, in_vmem = pl.BlockSpec(memory_space=pl.ANY), pl.BlockSpec(memory_space=pltpu.VMEM)
    scratch = (
        [vmem(129 * 16, UNIT, FIN), vmem(FIN, HID), vmem(2, SLOTS, TILE, TILE), vmem(256, HID)]
        + [vmem(2, SLOTS, dtype=I32)] * 2
        + [pltpu.SMEM((2, SLOTS), I32)] * 2
        + [vmem(256, HID)]
        + [vmem(4, 2, SLOTS, dtype=I32), pltpu.SMEM((4, 2, SLOTS), I32)]
        + [vmem(2, 8, TILE, dtype=I32)] * 3
        + [pltpu.SMEM((4, 8, TILE), I32)]
        + three(NONE + 1, rows=ROWS)
        + three(CHUNKS, rows=CHUNK)
        + three(2, 4, rows=CHUNK)
        + three(2, 4, rows=CHUNK)
        + three(4, 4, rows=CHUNK)
        + three(4, 4, rows=CHUNK)
        + three(4, 4, rows=CHUNK)
        + three(3, 4, rows=CHUNK)
        + three(4, rows=CHUNK)
        + three(3, rows=CHUNK)
        + [vmem(2 * FIN, TILE, dtype=F32)] * 2
        + [dma((13,)), dma, dma((3,))]
        + [dma((3, 3)), dma((3, 3)), dma((3, 12)), dma((3, 12)), dma((3, 8)), dma((3, 8))]
        + [dma((3, 12)), dma((3, 12)), dma((3, 16)), dma((3,))]
        + [dma((3, 4)), dma((3, 4)), dma((2,)), dma((2,)), dma((3, 4)), dma((3, 4)), dma((3, 8)), dma((3, 8))]
        + [dma((3, 3)), dma((3, 3)), dma((3, 3)), dma((3, 3))]
    )
    return pl.pallas_call(
        kernel,
        out_shape=(
            jax.ShapeDtypeStruct((256, HID), BF16),
            jax.ShapeDtypeStruct((256, FIN), F32),
            jax.ShapeDtypeStruct((1, HID), F32),
        ),
        in_specs=[anywhere] * 6,
        out_specs=(anywhere, in_vmem, in_vmem),
        scratch_shapes=scratch,
        compiler_params=pltpu.CompilerParams(
            collective_id=0, has_side_effects=True, vmem_limit_bytes=56 << 20
        ),
        name="graph_layer",
    )(features.reshape(16, UNIT, FIN), weight, tile_values, tile_cols, tile_counts, cotangent)


def solution(mesh):
    return jax.shard_map(
        on_device,
        mesh=mesh,
        in_specs=(
            P("dev", None),
            P(),
            P("dev", None, None, None),
            P("dev", None),
            P("dev", None),
            P("dev", None),
        ),
        out_specs=(P("dev", None), P("dev", None), P("dev", None)),
        check_vma=False,
    )
```

```python
import jax
import jax.numpy as jnp
from jax import lax
from jax.experimental import pallas as pl
from jax.experimental.pallas import tpu as pltpu
from jax.sharding import PartitionSpec as P

MESH = pl.DeviceIdType.MESH
BF16, F32, I32 = jnp.bfloat16, jnp.float32, jnp.int32
SIDE = 4
TILE, SLOTS, FIN, HID = 128, 32, 128, 256
CHUNKS = 64
UNIT = 16
UNITS = (6, 5, 5)
BASE = (0, 129 * 6, 129 * 11)
ROWS = (48, 48, 32)
STARTS = (0, 48, 96)
EXTRA = 16
CHUNK = (96, 96, 80)
NONE = 4 * SLOTS
ORDER = ((0, 1, 2), (1, 2, 0), (2, 0, 1))
HOPS = (1, 3, 2)


def pick(which, values):
    return jnp.where(which == 0, values[0], jnp.where(which == 1, values[1], values[2]))


def kernel(
    features_hbm, weight_hbm, tiles_hbm, cols_hbm, counts_hbm, cotangent_hbm,
    act_ref, grad_ref, weight_grad_ref,
    gathered, w_ref, tiles, ct_ref, cols_ref, counts_ref, cols_smem, counts_smem,
    place_ref, place_smem, slot_ref, twin_slot_out, twin_slot_ref, slot_smem, t0, t1, t2, own0, own1, own2,
    pass_up0, pass_up1, pass_up2, pass_down0, pass_down1, pass_down2,
    end0, end1, end2,
    b0, b1, b2, rb0, rb1, rb2, c0, c1, c2, rc0, rc1, rc2, wg_ref, twin_wg_ref,
    load_sem, table_sem, gs, g1r, g2r, gor, g3r, gcr, ts, tr, es, er, rs, par, per, br, cr,
):
    parts = range(3)
    terms, own = (t0, t1, t2), (own0, own1, own2)
    pass_up, pass_down = (pass_up0, pass_up1, pass_up2), (pass_down0, pass_down1, pass_down2)
    end = (end0, end1, end2)
    mid, mid_in = (b0, b1, b2), (rb0, rb1, rb2)
    last, last_in = (c0, c1, c2), (rc0, rc1, rc2)

    me = lax.axis_index("dev")
    core = me % 2
    at = (me // 32, (me // 8) % 4, (me // 2) % 4)
    strides = (32, 8, 2)

    def device(axis, hop):
        return (me + ((at[axis] + hop) % SIDE - at[axis]) * strides[axis],)

    twin = (me + 1 - 2 * core,)

    barrier = pltpu.get_barrier_semaphore()
    for hop in (2, 1, 3):
        for axis in range(3):
            pl.semaphore_signal(barrier, inc=1, device_id=device(axis, hop), device_id_type=MESH)
    pl.semaphore_signal(barrier, inc=1, device_id=twin, device_id_type=MESH)

    turn = [(core + p) % 3 for p in parts]
    i3, i2, i1 = ([pick((turn[p] + n) % 3, at) for p in parts] for n in range(3))
    s3, s2, s1 = ([pick((turn[p] + n) % 3, strides) for p in parts] for n in range(3))

    def move(index, stride, hop):
        return (me + ((index + hop) % SIDE - index) * stride,)

    def chunk(p, slow, middle, fast, count=1):
        at_chunk = core * CHUNKS + (slow * SIDE + middle) * SIDE + fast
        return gathered.at[pl.ds(BASE[p] + at_chunk * UNITS[p], count * UNITS[p])]

    loads = []

    def load(src, dst, n):
        copy = pltpu.make_async_copy(src, dst, load_sem.at[n])
        copy.start()
        loads.append(copy)

    for p, first, unit, count in ((0, 0, 0, 3), (1, 3, 0, 3), (2, 6, 0, 2), (0, 8, 3, 3), (1, 11, 3, 2), (2, 13, 2, 3)):
        place = BASE[p] + (core * CHUNKS + (i3[p] * SIDE + i2[p]) * SIDE + i1[p]) * UNITS[p] + unit
        load(features_hbm.at[pl.ds(first, count)], gathered.at[pl.ds(place, count)], 0)
    load(cols_hbm, cols_smem, 1)
    load(counts_hbm, counts_smem, 2)
    load(cols_hbm, cols_ref, 3)
    load(counts_hbm, counts_ref, 4)
    load(tiles_hbm, tiles, 5)
    load(weight_hbm, w_ref, 6)
    load(cotangent_hbm, ct_ref, 7)

    def send(src, dst, ssem, rsem, to):
        copy = pltpu.make_async_remote_copy(
            src_ref=src, dst_ref=dst, send_sem=ssem, recv_sem=rsem, device_id=to, device_id_type=MESH
        )
        copy.start()

    def arrived(dst, rsem):
        pltpu.make_async_remote_copy(
            src_ref=dst, dst_ref=dst, send_sem=es.at[0], recv_sem=rsem, device_id=twin, device_id_type=MESH
        ).wait_recv()

    def sent(src, ssem):
        pltpu.make_async_remote_copy(
            src_ref=src, dst_ref=src, send_sem=ssem, recv_sem=er.at[0], device_id=twin, device_id_type=MESH
        ).wait_send()

    pltpu.make_async_copy(features_hbm, gathered.at[pl.ds(0, 16)], load_sem.at[0]).wait()
    pl.semaphore_wait(barrier, 10)

    def first_sends(p, r):
        fast = i1[p] if r == 0 else (i1[p] + SIDE - HOPS[r - 1]) % SIDE
        ref = chunk(p, i3[p], i2[p], fast)
        if r > 0:
            arrived(ref, g1r.at[p, r - 1])
        for n, hop in enumerate(HOPS):
            send(ref, ref, gs.at[p], g2r.at[p, n], move(i2[p], s2[p], hop))
        return ref

    for p in parts:
        mine = chunk(p, i3[p], i2[p], i1[p])
        for n, hop in enumerate(HOPS):
            send(mine, mine, gs.at[p], g1r.at[p, n], move(i1[p], s1[p], hop))
    for r in range(4):
        refs = [first_sends(p, r) for p in parts]
        for p in parts:
            for n, hop in enumerate((1, 3)):
                send(refs[p], refs[p], gs.at[p], gor.at[p, n], move(i3[p], s3[p], hop))

    def slab(p, slow, r):
        middle = i2[p] if r == 0 else (i2[p] + SIDE - HOPS[r - 1]) % SIDE
        return chunk(p, slow, middle, 0, SIDE)

    def to_the_twin(p, ref, n):
        send(ref, ref, gs.at[p], gcr.at[p], twin)

    def slab_arrived(p, r, slow, n):
        ref = slab(p, slow, r)
        arrived(ref, gor.at[p, n] if r == 0 else g3r.at[p, 2 * (r - 1) + n])
        return ref

    def pass_on(p, r):
        up = slab_arrived(p, r, (i3[p] + 3) % SIDE, 0)
        if r < 2:
            send(up, up, gs.at[p], g3r.at[p, 6 + r], move(i3[p], s3[p], 1))
        to_the_twin(p, up, 4 + 2 * r)
        down = slab_arrived(p, r, (i3[p] + 1) % SIDE, 1)
        if r >= 2:
            send(down, down, gs.at[p], g3r.at[p, 6 + r], move(i3[p], s3[p], 3))
        to_the_twin(p, down, 5 + 2 * r)

    for p in parts:
        to_the_twin(p, slab(p, i3[p], 0), 0)

    for p in parts:
        gathered[pl.ds(BASE[p] + 2 * CHUNKS * UNITS[p], UNITS[p])] = jnp.zeros((UNITS[p], UNIT, FIN), BF16)
        terms[p][NONE] = jnp.zeros((ROWS[p], TILE), BF16)
    for copy in loads[6:]:
        copy.wait()
    cols = cols_ref[...]
    live = counts_ref[...] > 0
    where = (cols >> 6, (cols >> 4) & 3, (cols >> 2) & 3)
    col_core, half = (cols >> 1) & 1, jnp.where(live, cols & 1, 0)
    starts = []
    for p in parts:
        turned = (col_core + p) % 3
        flat = col_core
        for n in range(3):
            flat = flat * SIDE + pick((turned + n) % 3, where)
        starts.append(BASE[p] + jnp.where(live, flat, 2 * CHUNKS) * UNITS[p])
    place_ref[0] = starts[0] + 3 * half
    place_ref[1] = starts[1] + 3 * half
    place_ref[2] = jnp.where(half == 0, starts[1], starts[2]) + 2
    place_ref[3] = starts[2] + 3 * half
    place_copy = pltpu.make_async_copy(place_ref, place_smem, table_sem.at[0])
    place_copy.start()
    line = lax.broadcasted_iota(I32, (8, TILE), 0)
    lane = lax.broadcasted_iota(I32, (8, TILE), 1)
    digits = (lane >> 5, (lane >> 3) & 3, (lane >> 1) & 3)
    column = 0
    for axis in range(3):
        digit = pick(line & 3, [digits[ORDER[p].index(axis)] for p in parts])
        column = column * SIDE + digit
    column = column * 4 + (line >> 2) * 2 + (lane & 1)
    for b in range(2):
        def find(s, found, b=b):
            wanted = jnp.where(counts_smem[b, s] > 0, cols_smem[b, s], -1)
            return jnp.where(column == wanted, b * SLOTS + s, found)

        found = lax.fori_loop(0, SLOTS, find, jnp.full((8, TILE), NONE, I32))
        slot_ref[b] = found
        twin_slot_out[b] = jnp.where(found < NONE, found + 2 * SLOTS, NONE)
    send(twin_slot_out, twin_slot_ref, es.at[0], er.at[0], twin)
    slot_copy = pltpu.make_async_copy(slot_ref, slot_smem.at[pl.ds(0, 2)], table_sem.at[1])
    slot_copy.start()

    for r in range(1, 4):
        for p in parts:
            ref = slab(p, i3[p], r)
            arrived(ref, g2r.at[p, r - 1])
            send(ref, ref, gs.at[p], g3r.at[p, 2 * r - 2], move(i3[p], s3[p], 1))
            send(ref, ref, gs.at[p], g3r.at[p, 2 * r - 1], move(i3[p], s3[p], 3))
            to_the_twin(p, ref, r)
        for p in parts:
            pass_on(p, r - 1)
    for p in parts:
        pass_on(p, 3)
    for r in range(4):
        for p in parts:
            ref = slab(p, (i3[p] + 2) % SIDE, r)
            arrived(ref, g3r.at[p, 6 + r])
            to_the_twin(p, ref, 12 + r)
    place_copy.wait()
    slot_copy.wait()
    arrived(twin_slot_ref, er.at[0])
    twin_slot_copy = pltpu.make_async_copy(twin_slot_ref, slot_smem.at[pl.ds(2, 2)], table_sem.at[2])
    twin_slot_copy.start()
    for p in parts:
        arrived(
            gathered.at[pl.ds(BASE[p] + (1 - core) * CHUNKS * UNITS[p], CHUNKS * UNITS[p])], gcr.at[p]
        )

    def block_of(b, slot):
        pieces = [
            gathered[pl.ds(place_smem[0, b, slot], 3)].reshape(3 * UNIT, FIN),
            gathered[pl.ds(place_smem[1, b, slot], 2)].reshape(2 * UNIT, FIN),
            gathered[place_smem[2, b, slot]],
            gathered[pl.ds(place_smem[3, b, slot], 2)].reshape(2 * UNIT, FIN),
        ]
        return jnp.concatenate(pieces, axis=0)

    def forward_step(n, totals):
        new = []
        for b in range(2):
            total = totals[b]
            for k in range(FORWARD_UNROLL):
                slot = (n * FORWARD_UNROLL + k) * 2
                left = jnp.concatenate([tiles[b, slot], tiles[b, slot + 1]], axis=1)
                right = jnp.concatenate([block_of(b, slot), block_of(b, slot + 1)], axis=0)
                total = total + jnp.dot(left, right, preferred_element_type=F32)
            new.append(total)
        return tuple(new)

    zero = jnp.zeros((TILE, FIN), F32)
    totals = lax.fori_loop(0, SLOTS // (2 * FORWARD_UNROLL), forward_step, (zero, zero))
    aggregated = jnp.concatenate(totals, axis=0).astype(BF16)
    weight = w_ref[...]
    pre = jnp.dot(aggregated, weight, preferred_element_type=F32)
    sigma = jax.nn.sigmoid(pre)
    act_ref[...] = (pre * sigma).astype(BF16)
    delta = (ct_ref[...].astype(F32) * sigma * (1.0 + pre * (1.0 - sigma))).astype(BF16)
    back = lax.dot_general(
        weight, delta, (((1,), (1,)), ((), ())), preferred_element_type=F32
    ).astype(BF16)

    for b in range(2):
        left_factor = back[:, b * TILE : (b + 1) * TILE]
        for group in range(2):
            def term_step(n, carry, b=b, group=group, left_factor=left_factor):
                for k in range(TERM_UNROLL):
                    slot = group * 16 + (n * TERM_UNROLL + k) * 2
                    right = jnp.concatenate([tiles[b, slot], tiles[b, slot + 1]], axis=1)
                    both = jnp.dot(left_factor, right, preferred_element_type=F32).astype(BF16)
                    for which in range(2):
                        for p in parts:
                            terms[p][b * SLOTS + slot + which] = both[
                                STARTS[p] : STARTS[p] + ROWS[p], which * TILE : (which + 1) * TILE
                            ]
                return carry

            lax.fori_loop(0, 8 // TERM_UNROLL, term_step, 0)
            for p in parts:
                first = b * SLOTS + group * 16
                send(
                    terms[p].at[pl.ds(first, 16)], terms[p].at[pl.ds(2 * SLOTS + first, 16)],
                    ts.at[p], tr.at[p], twin,
                )
    weight_terms = lax.dot_general(
        aggregated, delta, (((0,), (0,)), ((), ())), preferred_element_type=F32
    )
    for which in range(2):
        wg_ref[pl.ds(which * FIN, FIN), :] = weight_terms[:, which * TILE : (which + 1) * TILE]
    send(wg_ref, twin_wg_ref, es.at[1], er.at[1], twin)
    twin_slot_copy.wait()
    for p in parts:
        arrived(terms[p].at[pl.ds(2 * SLOTS, 2 * SLOTS)], tr.at[p])
    arrived(twin_wg_ref, er.at[1])

    row = lax.broadcasted_iota(I32, (EXTRA, TILE), 0)

    def weight_rows(p, slow, middle, fast):
        moved = {ORDER[p][0]: slow, ORDER[p][1]: middle, ORDER[p][2]: fast}
        target = ((moved[0] * SIDE + moved[1]) * SIDE + moved[2]) * 2 + core
        rows = []
        for which in range(2):
            place = pl.ds(which * FIN + target, 1)
            rows.append(wg_ref[place, :] + twin_wg_ref[place, :])
        return jnp.where(row == 0, rows[0], jnp.where(row == 1, rows[1], 0.0)).astype(BF16)

    def spread(p, slow, middle, dst, extras):
        values = []
        for fast in range(SIDE):
            halves = []
            for which in range(2):
                entry = ((slow * SIDE + middle) * SIDE + fast) * 2 + which
                found = [terms[p][slot_smem[k, core * 4 + p, entry]] for k in range(4)]
                halves.append((found[0] + found[1]) + (found[2] + found[3]))
            if p == 2:
                halves.append(weight_rows(p, slow, middle, fast))
            value = jnp.concatenate(halves, axis=0)
            if extras:
                value = value.astype(F32)
                for extra in extras:
                    value = value + extra[fast].astype(F32)
                value = value.astype(BF16)
            values.append(value)
        for fast in range(SIDE):
            dst[fast] = values[fast]

    away = (2, 1, 3, 0)

    def middle_at(p, q):
        return (at[ORDER[p][1]] + away[q]) % SIDE

    def own_slab(p, o, q, extras=()):
        slow, middle = (at[ORDER[p][0]] + o) % SIDE, middle_at(p, q)
        ref = own[p].at[pl.ds((slow * SIDE + middle) * SIDE, SIDE)]
        spread(p, slow, middle, ref, extras)
        return ref

    up = [device(ORDER[p][0], 1) for p in parts]
    down = [device(ORDER[p][0], 3) for p in parts]
    for q in (0, 2, 1, 3):
        for p in parts:
            ref = own_slab(p, 2, q)
            if q < 2:
                send(ref, pass_up[p].at[q], rs.at[p], par.at[p, q], up[p])
            else:
                send(ref, pass_down[p].at[q - 2], rs.at[p], par.at[p, q], down[p])
    for q in range(2):
        for p in parts:
            send(own_slab(p, 1, q + 2), end[p].at[q + 2, 0], rs.at[p], per.at[p, q + 2], up[p])
            send(own_slab(p, 3, q), end[p].at[q, 1], rs.at[p], per.at[p, q], down[p])
    for q in range(2):
        for p in parts:
            arrived(pass_up[p].at[q], par.at[p, q])
            ref = own_slab(p, 1, q, (pass_up[p].at[q],))
            send(ref, end[p].at[q, 0], rs.at[p], per.at[p, q], up[p])
            arrived(pass_down[p].at[q], par.at[p, 2 + q])
            ref = own_slab(p, 3, q + 2, (pass_down[p].at[q],))
            send(ref, end[p].at[q + 2, 1], rs.at[p], per.at[p, q + 2], down[p])
    for q in range(4):
        for p in parts:
            arrived(end[p].at[q], per.at[p, q])
            spread(p, at[ORDER[p][0]], middle_at(p, q), mid[p].at[q], (end[p].at[q, 0], end[p].at[q, 1]))
            if q < 3:
                send(mid[p].at[q], mid_in[p].at[q], rs.at[p], br.at[p], device(ORDER[p][1], away[q]))
    for p in parts:
        arrived(mid_in[p], br.at[p])
        total = mid[p][3].astype(F32)
        for q in range(3):
            total = total + mid_in[p][q].astype(F32)
        last[p][...] = total.astype(BF16)
        for q in range(3):
            place = (at[ORDER[p][2]] + away[q]) % SIDE
            send(last[p].at[place], last_in[p].at[q], rs.at[p], cr.at[p], device(ORDER[p][2], away[q]))
    results = []
    for p in parts:
        arrived(last_in[p], cr.at[p])
        total = last[p][at[ORDER[p][2]]].astype(F32)
        for q in range(3):
            total = total + last_in[p][q].astype(F32)
        results.append(total)
    for which in range(2):
        block = jnp.concatenate(
            [results[p][which * ROWS[p] : (which + 1) * ROWS[p]] for p in parts], axis=0
        )
        grad_ref[pl.ds(which * TILE, TILE), :] = block.T
    weight_grad_ref[:, pl.ds(0, TILE)] = results[2][64:65]
    weight_grad_ref[:, pl.ds(TILE, TILE)] = results[2][65:66]
    for p in parts:
        sent(gathered.at[pl.ds(BASE[p], 127 * UNITS[p])], gs.at[p])
        sent(terms[p].at[pl.ds(0, 2 * SLOTS)], ts.at[p])
        sent(own[p].at[pl.ds(0, 63)], rs.at[p])
    sent(twin_slot_out, es.at[0])
    sent(wg_ref, es.at[1])


def hand_over(act_in, grad_in, weight_grad_in, act_ref, grad_ref, weight_grad_ref):
    act_ref[...] = act_in[...]
    grad_ref[...] = grad_in[...]
    weight_grad_ref[...] = weight_grad_in[...]


FORWARD_UNROLL = 4
TERM_UNROLL = 4


def on_device(features, weight, tile_values, tile_cols, tile_counts, cotangent):
    def vmem(*shape, dtype=BF16):
        return pltpu.VMEM(shape, dtype)

    def three(*lead, rows):
        return [vmem(*lead, rows[p], TILE) for p in range(3)]

    dma = pltpu.SemaphoreType.DMA
    in_hbm, in_vmem = pl.BlockSpec(memory_space=pltpu.HBM), pl.BlockSpec(memory_space=pltpu.VMEM)
    scratch = (
        [vmem(129 * 16, UNIT, FIN), vmem(FIN, HID), vmem(2, SLOTS, TILE, TILE), vmem(256, HID)]
        + [vmem(2, SLOTS, dtype=I32)] * 2
        + [pltpu.SMEM((2, SLOTS), I32)] * 2
        + [vmem(4, 2, SLOTS, dtype=I32), pltpu.SMEM((4, 2, SLOTS), I32)]
        + [vmem(2, 8, TILE, dtype=I32)] * 3
        + [pltpu.SMEM((4, 8, TILE), I32)]
        + three(NONE + 1, rows=ROWS)
        + three(CHUNKS, rows=CHUNK)
        + three(2, 4, rows=CHUNK)
        + three(2, 4, rows=CHUNK)
        + three(4, 2, 4, rows=CHUNK)
        + three(4, 4, rows=CHUNK)
        + three(3, 4, rows=CHUNK)
        + three(4, rows=CHUNK)
        + three(3, rows=CHUNK)
        + [vmem(2 * FIN, TILE, dtype=F32)] * 2
        + [dma((8,)), dma((3,)), dma((3,)), dma((3, 3)), dma((3, 3)), dma((3, 2)), dma((3, 10)), dma((3,))]
        + [dma((3,)), dma((3,)), dma((2,)), dma((2,)), dma((3,)), dma((3, 4)), dma((3, 4)), dma((3,)), dma((3,))]
    )
    shapes = (
        jax.ShapeDtypeStruct((256, HID), BF16),
        jax.ShapeDtypeStruct((256, FIN), F32),
        jax.ShapeDtypeStruct((1, HID), F32),
    )
    results = pl.pallas_call(
        kernel,
        out_shape=shapes,
        in_specs=[in_hbm] * 6,
        out_specs=(in_vmem,) * 3,
        scratch_shapes=scratch,
        compiler_params=pltpu.CompilerParams(
            collective_id=0, has_side_effects=True, vmem_limit_bytes=48 << 20
        ),
        name="graph_layer",
    )(*(
        pltpu.with_memory_space_constraint(x, pltpu.HBM)
        for x in (features.reshape(16, UNIT, FIN), weight, tile_values, tile_cols, tile_counts, cotangent)
    ))
    return pl.pallas_call(
        hand_over,
        out_shape=shapes,
        in_specs=[in_vmem] * 3,
        out_specs=(in_vmem,) * 3,
        compiler_params=pltpu.CompilerParams(vmem_limit_bytes=4 << 20),
        name="hand_over",
    )(*results)


def solution(mesh):
    return jax.shard_map(
        on_device,
        mesh=mesh,
        in_specs=(
            P("dev", None),
            P(),
            P("dev", None, None, None),
            P("dev", None),
            P("dev", None),
            P("dev", None),
        ),
        out_specs=(P("dev", None), P("dev", None), P("dev", None)),
        check_vma=False,
    )
```

```python
import jax
import jax.numpy as jnp
from jax import lax
from jax.experimental import pallas as pl
from jax.experimental.pallas import tpu as pltpu
from jax.sharding import PartitionSpec as P

MESH = pl.DeviceIdType.MESH
BF16, F32, I32 = jnp.bfloat16, jnp.float32, jnp.int32
SIDE = 4
TILE, SLOTS, FIN, HID = 128, 32, 128, 256
CHUNKS = 64
UNIT = 16
UNITS = (6, 5, 5)
BASE = (0, 129 * 6, 129 * 11)
ROWS = (48, 48, 32)
STARTS = (0, 48, 96)
EXTRA = 16
CHUNK = (96, 96, 80)
NONE = 4 * SLOTS
ORDER = ((0, 1, 2), (1, 2, 0), (2, 0, 1))
HOPS = (1, 3, 2)


def pick(which, values):
    return jnp.where(which == 0, values[0], jnp.where(which == 1, values[1], values[2]))


def kernel(
    features_hbm, weight_hbm, tiles_hbm, cols_hbm, counts_hbm, cotangent_hbm,
    act_ref, grad_ref, weight_grad_ref,
    gathered, w_ref, tiles, ct_ref, cols_ref, counts_ref, cols_smem, counts_smem,
    place_ref, place_smem, slot_ref, twin_slot_out, twin_slot_ref, slot_smem, t0, t1, t2, own0, own1, own2,
    pass_up0, pass_up1, pass_up2, pass_down0, pass_down1, pass_down2,
    end0, end1, end2,
    b0, b1, b2, rb0, rb1, rb2, c0, c1, c2, rc0, rc1, rc2, wg_ref, twin_wg_ref,
    load_sem, table_sem, gs, g1r, g2r, g3r, gfr, gcr, ts, tr, es, er, rs, par, per, br, cr,
):
    parts = range(3)
    terms, own = (t0, t1, t2), (own0, own1, own2)
    pass_up, pass_down = (pass_up0, pass_up1, pass_up2), (pass_down0, pass_down1, pass_down2)
    end = (end0, end1, end2)
    mid, mid_in = (b0, b1, b2), (rb0, rb1, rb2)
    last, last_in = (c0, c1, c2), (rc0, rc1, rc2)

    me = lax.axis_index("dev")
    core = me % 2
    at = (me // 32, (me // 8) % 4, (me // 2) % 4)
    strides = (32, 8, 2)

    def device(axis, hop):
        return (me + ((at[axis] + hop) % SIDE - at[axis]) * strides[axis],)

    twin = (me + 1 - 2 * core,)

    barrier = pltpu.get_barrier_semaphore()
    for hop in (2, 1, 3):
        for axis in range(3):
            pl.semaphore_signal(barrier, inc=1, device_id=device(axis, hop), device_id_type=MESH)
    pl.semaphore_signal(barrier, inc=1, device_id=twin, device_id_type=MESH)

    turn = [(core + p) % 3 for p in parts]
    i3, i2, i1 = ([pick((turn[p] + n) % 3, at) for p in parts] for n in range(3))
    s3, s2, s1 = ([pick((turn[p] + n) % 3, strides) for p in parts] for n in range(3))

    def move(index, stride, hop):
        return (me + ((index + hop) % SIDE - index) * stride,)

    def chunk(p, slow, fast, middle, count=1):
        at_chunk = core * CHUNKS + (slow * SIDE + fast) * SIDE + middle
        return gathered.at[pl.ds(BASE[p] + at_chunk * UNITS[p], count * UNITS[p])]

    loads = []

    def load(src, dst, n):
        copy = pltpu.make_async_copy(src, dst, load_sem.at[n])
        copy.start()
        loads.append(copy)

    for p, first, unit, count in ((0, 0, 0, 3), (1, 3, 0, 3), (2, 6, 0, 2), (0, 8, 3, 3), (1, 11, 3, 2), (2, 13, 2, 3)):
        place = BASE[p] + (core * CHUNKS + (i3[p] * SIDE + i1[p]) * SIDE + i2[p]) * UNITS[p] + unit
        load(features_hbm.at[pl.ds(first, count)], gathered.at[pl.ds(place, count)], 0)
    load(cols_hbm, cols_smem, 1)
    load(counts_hbm, counts_smem, 2)
    load(cols_hbm, cols_ref, 3)
    load(counts_hbm, counts_ref, 4)
    load(tiles_hbm, tiles, 5)
    load(weight_hbm, w_ref, 6)
    load(cotangent_hbm, ct_ref, 7)

    def send(src, dst, ssem, rsem, to):
        copy = pltpu.make_async_remote_copy(
            src_ref=src, dst_ref=dst, send_sem=ssem, recv_sem=rsem, device_id=to, device_id_type=MESH
        )
        copy.start()

    def arrived(dst, rsem):
        pltpu.make_async_remote_copy(
            src_ref=dst, dst_ref=dst, send_sem=es.at[0], recv_sem=rsem, device_id=twin, device_id_type=MESH
        ).wait_recv()

    def sent(src, ssem):
        pltpu.make_async_remote_copy(
            src_ref=src, dst_ref=src, send_sem=ssem, recv_sem=er.at[0], device_id=twin, device_id_type=MESH
        ).wait_send()

    pltpu.make_async_copy(features_hbm, gathered.at[pl.ds(0, 16)], load_sem.at[0]).wait()
    pl.semaphore_wait(barrier, 10)

    def fast_at(p, r):
        return i1[p] if r == 0 else (i1[p] + SIDE - HOPS[r - 1]) % SIDE

    def along_third(p, r, ref):
        for n, hop in enumerate((1, 3)):
            send(ref, ref, gs.at[p], g3r.at[p, 2 * r + n], move(i3[p], s3[p], hop))

    def first_sends(p, r):
        ref = chunk(p, i3[p], fast_at(p, r), i2[p])
        if r > 0:
            arrived(ref, g1r.at[p, r - 1])
        for n, hop in enumerate(HOPS):
            send(ref, ref, gs.at[p], g2r.at[p, r * 3 + n], move(i2[p], s2[p], hop))
        return ref

    for p in parts:
        mine = chunk(p, i3[p], i1[p], i2[p])
        for n, hop in enumerate(HOPS):
            send(mine, mine, gs.at[p], g1r.at[p, n], move(i1[p], s1[p], hop))
    for r in range(4):
        refs = [first_sends(p, r) for p in parts]
        for p in parts:
            along_third(p, r, refs[p])

    def group(p, slow, r, first=0, count=SIDE):
        return chunk(p, slow, fast_at(p, r), first, count)

    def to_the_twin(p, ref):
        send(ref, ref, gs.at[p], gcr.at[p], twin)

    def last_sends(p, r):
        for n, hop in enumerate(HOPS):
            ref = chunk(p, i3[p], fast_at(p, r), (i2[p] + SIDE - hop) % SIDE)
            arrived(ref, g2r.at[p, r * 3 + n])
            along_third(p, r, ref)
        to_the_twin(p, group(p, i3[p], r))

    def pass_on(p, r):
        below, above = (i3[p] + 3) % SIDE, (i3[p] + 1) % SIDE
        arrived(group(p, below, r), g3r.at[p, 2 * r])
        half = group(p, below, r, 0, 2)
        send(half, half, gs.at[p], gfr.at[p, r], move(i3[p], s3[p], 1))
        arrived(group(p, above, r), g3r.at[p, 2 * r + 1])
        half = group(p, above, r, 2, 2)
        send(half, half, gs.at[p], gfr.at[p, r], move(i3[p], s3[p], 3))
        to_the_twin(p, group(p, below, r))
        to_the_twin(p, group(p, above, r))

    def opposite(p, r):
        ref = group(p, (i3[p] + 2) % SIDE, r)
        arrived(ref, gfr.at[p, r])
        to_the_twin(p, ref)

    for p in parts:
        last_sends(p, 0)
    for p in parts:
        gathered[pl.ds(BASE[p] + 2 * CHUNKS * UNITS[p], UNITS[p])] = jnp.zeros((UNITS[p], UNIT, FIN), BF16)
        terms[p][NONE] = jnp.zeros((ROWS[p], TILE), BF16)
    for copy in loads[6:]:
        copy.wait()
    cols = cols_ref[...]
    live = counts_ref[...] > 0
    where = (cols >> 6, (cols >> 4) & 3, (cols >> 2) & 3)
    col_core, half = (cols >> 1) & 1, jnp.where(live, cols & 1, 0)
    starts = []
    for p in parts:
        turned = (col_core + p) % 3
        flat = col_core
        for n in (0, 2, 1):
            flat = flat * SIDE + pick((turned + n) % 3, where)
        starts.append(BASE[p] + jnp.where(live, flat, 2 * CHUNKS) * UNITS[p])
    place_ref[0] = starts[0] + 3 * half
    place_ref[1] = starts[1] + 3 * half
    place_ref[2] = jnp.where(half == 0, starts[1], starts[2]) + 2
    place_ref[3] = starts[2] + 3 * half
    place_copy = pltpu.make_async_copy(place_ref, place_smem, table_sem.at[0])
    place_copy.start()
    line = lax.broadcasted_iota(I32, (8, TILE), 0)
    lane = lax.broadcasted_iota(I32, (8, TILE), 1)
    digits = (lane >> 5, (lane >> 3) & 3, (lane >> 1) & 3)
    column = 0
    for axis in range(3):
        digit = pick(line & 3, [digits[ORDER[p].index(axis)] for p in parts])
        column = column * SIDE + digit
    column = column * 4 + (line >> 2) * 2 + (lane & 1)
    for b in range(2):
        def find(s, found, b=b):
            wanted = jnp.where(counts_smem[b, s] > 0, cols_smem[b, s], -1)
            return jnp.where(column == wanted, b * SLOTS + s, found)

        found = lax.fori_loop(0, SLOTS, find, jnp.full((8, TILE), NONE, I32))
        slot_ref[b] = found
        twin_slot_out[b] = jnp.where(found < NONE, found + 2 * SLOTS, NONE)
    send(twin_slot_out, twin_slot_ref, es.at[0], er.at[0], twin)
    slot_copy = pltpu.make_async_copy(slot_ref, slot_smem.at[pl.ds(0, 2)], table_sem.at[1])
    slot_copy.start()
    for p in parts:
        last_sends(p, 1)
    for p in parts:
        pass_on(p, 0)
    for p in parts:
        last_sends(p, 2)
    for p in parts:
        pass_on(p, 1)
    for p in parts:
        last_sends(p, 3)
    for r in range(2, 4):
        for p in parts:
            pass_on(p, r)
        for p in parts:
            opposite(p, r - 2)
    for r in range(2, 4):
        for p in parts:
            opposite(p, r)
    place_copy.wait()
    slot_copy.wait()
    arrived(twin_slot_ref, er.at[0])
    twin_slot_copy = pltpu.make_async_copy(twin_slot_ref, slot_smem.at[pl.ds(2, 2)], table_sem.at[2])
    twin_slot_copy.start()
    for p in parts:
        arrived(
            gathered.at[pl.ds(BASE[p] + (1 - core) * CHUNKS * UNITS[p], CHUNKS * UNITS[p])], gcr.at[p]
        )

    def block_of(b, slot):
        pieces = [
            gathered[pl.ds(place_smem[0, b, slot], 3)].reshape(3 * UNIT, FIN),
            gathered[pl.ds(place_smem[1, b, slot], 2)].reshape(2 * UNIT, FIN),
            gathered[place_smem[2, b, slot]],
            gathered[pl.ds(place_smem[3, b, slot], 2)].reshape(2 * UNIT, FIN),
        ]
        return jnp.concatenate(pieces, axis=0)

    def forward_step(n, totals):
        new = []
        for b in range(2):
            total = totals[b]
            for k in range(FORWARD_UNROLL):
                slot = (n * FORWARD_UNROLL + k) * 2
                left = jnp.concatenate([tiles[b, slot], tiles[b, slot + 1]], axis=1)
                right = jnp.concatenate([block_of(b, slot), block_of(b, slot + 1)], axis=0)
                total = total + jnp.dot(left, right, preferred_element_type=F32)
            new.append(total)
        return tuple(new)

    zero = jnp.zeros((TILE, FIN), F32)
    totals = lax.fori_loop(0, SLOTS // (2 * FORWARD_UNROLL), forward_step, (zero, zero))
    aggregated = jnp.concatenate(totals, axis=0).astype(BF16)
    weight = w_ref[...]
    pre = jnp.dot(aggregated, weight, preferred_element_type=F32)
    sigma = jax.nn.sigmoid(pre)
    act_ref[...] = (pre * sigma).astype(BF16)
    delta = (ct_ref[...].astype(F32) * sigma * (1.0 + pre * (1.0 - sigma))).astype(BF16)
    back = lax.dot_general(
        weight, delta, (((1,), (1,)), ((), ())), preferred_element_type=F32
    ).astype(BF16)

    for b in range(2):
        left_factor = back[:, b * TILE : (b + 1) * TILE]
        for group in range(2):
            def term_step(n, carry, b=b, group=group, left_factor=left_factor):
                for k in range(TERM_UNROLL):
                    slot = group * 16 + (n * TERM_UNROLL + k) * 2
                    right = jnp.concatenate([tiles[b, slot], tiles[b, slot + 1]], axis=1)
                    both = jnp.dot(left_factor, right, preferred_element_type=F32).astype(BF16)
                    for which in range(2):
                        for p in parts:
                            terms[p][b * SLOTS + slot + which] = both[
                                STARTS[p] : STARTS[p] + ROWS[p], which * TILE : (which + 1) * TILE
                            ]
                return carry

            lax.fori_loop(0, 8 // TERM_UNROLL, term_step, 0)
            for p in parts:
                first = b * SLOTS + group * 16
                send(
                    terms[p].at[pl.ds(first, 16)], terms[p].at[pl.ds(2 * SLOTS + first, 16)],
                    ts.at[p], tr.at[p], twin,
                )
    weight_terms = lax.dot_general(
        aggregated, delta, (((0,), (0,)), ((), ())), preferred_element_type=F32
    )
    for which in range(2):
        wg_ref[pl.ds(which * FIN, FIN), :] = weight_terms[:, which * TILE : (which + 1) * TILE]
    send(wg_ref, twin_wg_ref, es.at[1], er.at[1], twin)
    twin_slot_copy.wait()
    for p in parts:
        arrived(terms[p].at[pl.ds(2 * SLOTS, 2 * SLOTS)], tr.at[p])
    arrived(twin_wg_ref, er.at[1])

    row = lax.broadcasted_iota(I32, (EXTRA, TILE), 0)

    def weight_rows(p, slow, middle, fast):
        moved = {ORDER[p][0]: slow, ORDER[p][1]: middle, ORDER[p][2]: fast}
        target = ((moved[0] * SIDE + moved[1]) * SIDE + moved[2]) * 2 + core
        rows = []
        for which in range(2):
            place = pl.ds(which * FIN + target, 1)
            rows.append(wg_ref[place, :] + twin_wg_ref[place, :])
        return jnp.where(row == 0, rows[0], jnp.where(row == 1, rows[1], 0.0)).astype(BF16)

    def spread(p, slow, middle, dst, extras):
        values = []
        for fast in range(SIDE):
            halves = []
            for which in range(2):
                entry = ((slow * SIDE + middle) * SIDE + fast) * 2 + which
                found = [terms[p][slot_smem[k, core * 4 + p, entry]] for k in range(4)]
                halves.append((found[0] + found[1]) + (found[2] + found[3]))
            if p == 2:
                halves.append(weight_rows(p, slow, middle, fast))
            value = jnp.concatenate(halves, axis=0)
            if extras:
                value = value.astype(F32)
                for extra in extras:
                    value = value + extra[fast].astype(F32)
                value = value.astype(BF16)
            values.append(value)
        for fast in range(SIDE):
            dst[fast] = values[fast]

    away = (2, 1, 3, 0)

    def middle_at(p, q):
        return (at[ORDER[p][1]] + away[q]) % SIDE

    def own_slab(p, o, q, extras=()):
        slow, middle = (at[ORDER[p][0]] + o) % SIDE, middle_at(p, q)
        ref = own[p].at[pl.ds((slow * SIDE + middle) * SIDE, SIDE)]
        spread(p, slow, middle, ref, extras)
        return ref

    up = [device(ORDER[p][0], 1) for p in parts]
    down = [device(ORDER[p][0], 3) for p in parts]
    for q in (0, 2, 1, 3):
        for p in parts:
            ref = own_slab(p, 2, q)
            if q < 2:
                send(ref, pass_up[p].at[q], rs.at[p], par.at[p, q], up[p])
            else:
                send(ref, pass_down[p].at[q - 2], rs.at[p], par.at[p, q], down[p])
    for q in range(2):
        for p in parts:
            send(own_slab(p, 1, q + 2), end[p].at[q + 2, 0], rs.at[p], per.at[p, q + 2], up[p])
            send(own_slab(p, 3, q), end[p].at[q, 1], rs.at[p], per.at[p, q], down[p])
    for q in range(2):
        for p in parts:
            arrived(pass_up[p].at[q], par.at[p, q])
            ref = own_slab(p, 1, q, (pass_up[p].at[q],))
            send(ref, end[p].at[q, 0], rs.at[p], per.at[p, q], up[p])
            arrived(pass_down[p].at[q], par.at[p, 2 + q])
            ref = own_slab(p, 3, q + 2, (pass_down[p].at[q],))
            send(ref, end[p].at[q + 2, 1], rs.at[p], per.at[p, q + 2], down[p])
    for q in range(4):
        for p in parts:
            arrived(end[p].at[q], per.at[p, q])
            spread(p, at[ORDER[p][0]], middle_at(p, q), mid[p].at[q], (end[p].at[q, 0], end[p].at[q, 1]))
            if q < 3:
                send(mid[p].at[q], mid_in[p].at[q], rs.at[p], br.at[p], device(ORDER[p][1], away[q]))
    for p in parts:
        arrived(mid_in[p], br.at[p])
        total = mid[p][3].astype(F32)
        for q in range(3):
            total = total + mid_in[p][q].astype(F32)
        last[p][...] = total.astype(BF16)
        for q in range(3):
            place = (at[ORDER[p][2]] + away[q]) % SIDE
            send(last[p].at[place], last_in[p].at[q], rs.at[p], cr.at[p], device(ORDER[p][2], away[q]))
    results = []
    for p in parts:
        arrived(last_in[p], cr.at[p])
        total = last[p][at[ORDER[p][2]]].astype(F32)
        for q in range(3):
            total = total + last_in[p][q].astype(F32)
        results.append(total)
    for which in range(2):
        block = jnp.concatenate(
            [results[p][which * ROWS[p] : (which + 1) * ROWS[p]] for p in parts], axis=0
        )
        grad_ref[pl.ds(which * TILE, TILE), :] = block.T
    weight_grad_ref[:, pl.ds(0, TILE)] = results[2][64:65]
    weight_grad_ref[:, pl.ds(TILE, TILE)] = results[2][65:66]
    for p in parts:
        sent(gathered.at[pl.ds(BASE[p], 127 * UNITS[p])], gs.at[p])
        sent(terms[p].at[pl.ds(0, 2 * SLOTS)], ts.at[p])
        sent(own[p].at[pl.ds(0, 63)], rs.at[p])
    sent(twin_slot_out, es.at[0])
    sent(wg_ref, es.at[1])


def hand_over(act_in, grad_in, weight_grad_in, act_ref, grad_ref, weight_grad_ref):
    act_ref[...] = act_in[...]
    grad_ref[...] = grad_in[...]
    weight_grad_ref[...] = weight_grad_in[...]


FORWARD_UNROLL = 4
TERM_UNROLL = 4


def on_device(features, weight, tile_values, tile_cols, tile_counts, cotangent):
    def vmem(*shape, dtype=BF16):
        return pltpu.VMEM(shape, dtype)

    def three(*lead, rows):
        return [vmem(*lead, rows[p], TILE) for p in range(3)]

    dma = pltpu.SemaphoreType.DMA
    in_hbm, in_vmem = pl.BlockSpec(memory_space=pltpu.HBM), pl.BlockSpec(memory_space=pltpu.VMEM)
    scratch = (
        [vmem(129 * 16, UNIT, FIN), vmem(FIN, HID), vmem(2, SLOTS, TILE, TILE), vmem(256, HID)]
        + [vmem(2, SLOTS, dtype=I32)] * 2
        + [pltpu.SMEM((2, SLOTS), I32)] * 2
        + [vmem(4, 2, SLOTS, dtype=I32), pltpu.SMEM((4, 2, SLOTS), I32)]
        + [vmem(2, 8, TILE, dtype=I32)] * 3
        + [pltpu.SMEM((4, 8, TILE), I32)]
        + three(NONE + 1, rows=ROWS)
        + three(CHUNKS, rows=CHUNK)
        + three(2, 4, rows=CHUNK)
        + three(2, 4, rows=CHUNK)
        + three(4, 2, 4, rows=CHUNK)
        + three(4, 4, rows=CHUNK)
        + three(3, 4, rows=CHUNK)
        + three(4, rows=CHUNK)
        + three(3, rows=CHUNK)
        + [vmem(2 * FIN, TILE, dtype=F32)] * 2
        + [dma((8,)), dma((3,)), dma((3,)), dma((3, 3)), dma((3, 12)), dma((3, 8)), dma((3, 4)), dma((3,))]
        + [dma((3,)), dma((3,)), dma((2,)), dma((2,)), dma((3,)), dma((3, 4)), dma((3, 4)), dma((3,)), dma((3,))]
    )
    shapes = (
        jax.ShapeDtypeStruct((256, HID), BF16),
        jax.ShapeDtypeStruct((256, FIN), F32),
        jax.ShapeDtypeStruct((1, HID), F32),
    )
    results = pl.pallas_call(
        kernel,
        out_shape=shapes,
        in_specs=[in_hbm] * 6,
        out_specs=(in_vmem,) * 3,
        scratch_shapes=scratch,
        compiler_params=pltpu.CompilerParams(
            collective_id=0, has_side_effects=True, vmem_limit_bytes=48 << 20
        ),
        name="graph_layer",
    )(*(
        pltpu.with_memory_space_constraint(x, pltpu.HBM)
        for x in (features.reshape(16, UNIT, FIN), weight, tile_values, tile_cols, tile_counts, cotangent)
    ))
    return pl.pallas_call(
        hand_over,
        out_shape=shapes,
        in_specs=[in_vmem] * 3,
        out_specs=(in_vmem,) * 3,
        compiler_params=pltpu.CompilerParams(vmem_limit_bytes=4 << 20),
        name="hand_over",
    )(*results)


def solution(mesh):
    return jax.shard_map(
        on_device,
        mesh=mesh,
        in_specs=(
            P("dev", None),
            P(),
            P("dev", None, None, None),
            P("dev", None),
            P("dev", None),
            P("dev", None),
        ),
        out_specs=(P("dev", None), P("dev", None), P("dev", None)),
        check_vma=False,
    )
```

```python
import jax
import jax.numpy as jnp
from jax import lax
from jax.experimental import pallas as pl
from jax.experimental.pallas import tpu as pltpu
from jax.sharding import PartitionSpec as P

MESH = pl.DeviceIdType.MESH
BF16, F32, I32 = jnp.bfloat16, jnp.float32, jnp.int32
SIDE = 4
TILE, SLOTS, FIN, HID = 128, 32, 128, 256
CHUNKS = 64
UNIT = 16
UNITS = (6, 5, 5)
BASE = (0, 129 * 6, 129 * 11)
ROWS = (48, 48, 32)
STARTS = (0, 48, 96)
EXTRA = 16
CHUNK = (96, 96, 80)
NONE = 4 * SLOTS
ORDER = ((0, 1, 2), (1, 2, 0), (2, 0, 1))
HOPS = (1, 3, 2)


def pick(which, values):
    return jnp.where(which == 0, values[0], jnp.where(which == 1, values[1], values[2]))


def kernel(
    features_hbm, weight_hbm, tiles_hbm, cols_hbm, counts_hbm, cotangent_hbm,
    act_ref, grad_ref, weight_grad_ref,
    gathered, w_ref, tiles, ct_ref, cols_ref, counts_ref, cols_smem, counts_smem,
    place_ref, place_smem, slot_ref, twin_slot_out, twin_slot_ref, slot_smem, t0, t1, t2, own0, own1, own2,
    pass_up0, pass_up1, pass_up2, pass_down0, pass_down1, pass_down2,
    end0, end1, end2,
    b0, b1, b2, bp0, bp1, bp2, rb0, rb1, rb2, c0, c1, c2, rc0, rc1, rc2, wg_ref, twin_wg_ref,
    load_sem, table_sem, gs, g1r, g2r, g3r, gfr, gcr, ts, tr, es, er, rs, par, per, bpr, br, cr,
):
    parts = range(3)
    terms, own = (t0, t1, t2), (own0, own1, own2)
    pass_up, pass_down = (pass_up0, pass_up1, pass_up2), (pass_down0, pass_down1, pass_down2)
    end = (end0, end1, end2)
    mid, mid_pass, mid_in = (b0, b1, b2), (bp0, bp1, bp2), (rb0, rb1, rb2)
    last, last_in = (c0, c1, c2), (rc0, rc1, rc2)

    me = lax.axis_index("dev")
    core = me % 2
    at = (me // 32, (me // 8) % 4, (me // 2) % 4)
    strides = (32, 8, 2)

    def device(axis, hop):
        return (me + ((at[axis] + hop) % SIDE - at[axis]) * strides[axis],)

    twin = (me + 1 - 2 * core,)

    barrier = pltpu.get_barrier_semaphore()
    for hop in (2, 1, 3):
        for axis in range(3):
            pl.semaphore_signal(barrier, inc=1, device_id=device(axis, hop), device_id_type=MESH)
    pl.semaphore_signal(barrier, inc=1, device_id=twin, device_id_type=MESH)

    turn = [(core + p) % 3 for p in parts]
    i3, i2, i1 = ([pick((turn[p] + n) % 3, at) for p in parts] for n in range(3))
    s3, s2, s1 = ([pick((turn[p] + n) % 3, strides) for p in parts] for n in range(3))

    def move(index, stride, hop):
        return (me + ((index + hop) % SIDE - index) * stride,)

    def chunk(p, slow, fast, middle, count=1):
        at_chunk = core * CHUNKS + (slow * SIDE + fast) * SIDE + middle
        return gathered.at[pl.ds(BASE[p] + at_chunk * UNITS[p], count * UNITS[p])]

    loads = []

    def load(src, dst, n):
        copy = pltpu.make_async_copy(src, dst, load_sem.at[n])
        copy.start()
        loads.append(copy)

    for p, first, unit, count in ((0, 0, 0, 3), (1, 3, 0, 3), (2, 6, 0, 2), (0, 8, 3, 3), (1, 11, 3, 2), (2, 13, 2, 3)):
        place = BASE[p] + (core * CHUNKS + (i3[p] * SIDE + i1[p]) * SIDE + i2[p]) * UNITS[p] + unit
        load(features_hbm.at[pl.ds(first, count)], gathered.at[pl.ds(place, count)], 0)
    load(cols_hbm, cols_smem, 1)
    load(counts_hbm, counts_smem, 2)
    load(cols_hbm, cols_ref, 3)
    load(counts_hbm, counts_ref, 4)
    load(tiles_hbm, tiles, 5)
    load(weight_hbm, w_ref, 6)
    load(cotangent_hbm, ct_ref, 7)

    def send(src, dst, ssem, rsem, to):
        copy = pltpu.make_async_remote_copy(
            src_ref=src, dst_ref=dst, send_sem=ssem, recv_sem=rsem, device_id=to, device_id_type=MESH
        )
        copy.start()

    def arrived(dst, rsem):
        pltpu.make_async_remote_copy(
            src_ref=dst, dst_ref=dst, send_sem=es.at[0], recv_sem=rsem, device_id=twin, device_id_type=MESH
        ).wait_recv()

    def sent(src, ssem):
        pltpu.make_async_remote_copy(
            src_ref=src, dst_ref=src, send_sem=ssem, recv_sem=er.at[0], device_id=twin, device_id_type=MESH
        ).wait_send()

    pltpu.make_async_copy(features_hbm, gathered.at[pl.ds(0, 16)], load_sem.at[0]).wait()
    pl.semaphore_wait(barrier, 10)

    def fast_at(p, r):
        return i1[p] if r == 0 else (i1[p] + SIDE - HOPS[r - 1]) % SIDE

    def along_third(p, r, ref):
        for n, hop in enumerate((1, 3)):
            send(ref, ref, gs.at[p], g3r.at[p, 2 * r + n], move(i3[p], s3[p], hop))

    def first_sends(p, r):
        ref = chunk(p, i3[p], fast_at(p, r), i2[p])
        if r > 0:
            arrived(ref, g1r.at[p, r - 1])
        for n, hop in enumerate(HOPS):
            send(ref, ref, gs.at[p], g2r.at[p, r * 3 + n], move(i2[p], s2[p], hop))
        return ref

    for p in parts:
        mine = chunk(p, i3[p], i1[p], i2[p])
        for n, hop in enumerate(HOPS):
            send(mine, mine, gs.at[p], g1r.at[p, n], move(i1[p], s1[p], hop))
    for r in range(4):
        refs = [first_sends(p, r) for p in parts]
        for p in parts:
            along_third(p, r, refs[p])

    def group(p, slow, r, first=0, count=SIDE):
        return chunk(p, slow, fast_at(p, r), first, count)

    def to_the_twin(p, ref):
        send(ref, ref, gs.at[p], gcr.at[p], twin)

    def last_sends(p, r):
        for n, hop in enumerate(HOPS):
            ref = chunk(p, i3[p], fast_at(p, r), (i2[p] + SIDE - hop) % SIDE)
            arrived(ref, g2r.at[p, r * 3 + n])
            along_third(p, r, ref)
        to_the_twin(p, group(p, i3[p], r))

    def pass_on(p, r):
        below, above = (i3[p] + 3) % SIDE, (i3[p] + 1) % SIDE
        arrived(group(p, below, r), g3r.at[p, 2 * r])
        half = group(p, below, r, 0, 2)
        send(half, half, gs.at[p], gfr.at[p, r], move(i3[p], s3[p], 1))
        arrived(group(p, above, r), g3r.at[p, 2 * r + 1])
        half = group(p, above, r, 2, 2)
        send(half, half, gs.at[p], gfr.at[p, r], move(i3[p], s3[p], 3))
        to_the_twin(p, group(p, below, r))
        to_the_twin(p, group(p, above, r))

    def opposite(p, r):
        ref = group(p, (i3[p] + 2) % SIDE, r)
        arrived(ref, gfr.at[p, r])
        to_the_twin(p, ref)

    for p in parts:
        last_sends(p, 0)
    for p in parts:
        gathered[pl.ds(BASE[p] + 2 * CHUNKS * UNITS[p], UNITS[p])] = jnp.zeros((UNITS[p], UNIT, FIN), BF16)
        terms[p][NONE] = jnp.zeros((ROWS[p], TILE), BF16)
    for copy in loads[6:]:
        copy.wait()
    cols = cols_ref[...]
    live = counts_ref[...] > 0
    where = (cols >> 6, (cols >> 4) & 3, (cols >> 2) & 3)
    col_core, half = (cols >> 1) & 1, jnp.where(live, cols & 1, 0)
    starts = []
    for p in parts:
        turned = (col_core + p) % 3
        flat = col_core
        for n in (0, 2, 1):
            flat = flat * SIDE + pick((turned + n) % 3, where)
        starts.append(BASE[p] + jnp.where(live, flat, 2 * CHUNKS) * UNITS[p])
    place_ref[0] = starts[0] + 3 * half
    place_ref[1] = starts[1] + 3 * half
    place_ref[2] = jnp.where(half == 0, starts[1], starts[2]) + 2
    place_ref[3] = starts[2] + 3 * half
    place_copy = pltpu.make_async_copy(place_ref, place_smem, table_sem.at[0])
    place_copy.start()
    line = lax.broadcasted_iota(I32, (8, TILE), 0)
    lane = lax.broadcasted_iota(I32, (8, TILE), 1)
    digits = (lane >> 5, (lane >> 3) & 3, (lane >> 1) & 3)
    column = 0
    for axis in range(3):
        digit = pick(line & 3, [digits[ORDER[p].index(axis)] for p in parts])
        column = column * SIDE + digit
    column = column * 4 + (line >> 2) * 2 + (lane & 1)
    for b in range(2):
        def find(s, found, b=b):
            wanted = jnp.where(counts_smem[b, s] > 0, cols_smem[b, s], -1)
            return jnp.where(column == wanted, b * SLOTS + s, found)

        found = lax.fori_loop(0, SLOTS, find, jnp.full((8, TILE), NONE, I32))
        slot_ref[b] = found
        twin_slot_out[b] = jnp.where(found < NONE, found + 2 * SLOTS, NONE)
    send(twin_slot_out, twin_slot_ref, es.at[0], er.at[0], twin)
    slot_copy = pltpu.make_async_copy(slot_ref, slot_smem.at[pl.ds(0, 2)], table_sem.at[1])
    slot_copy.start()
    for p in parts:
        last_sends(p, 1)
    for p in parts:
        pass_on(p, 0)
    for p in parts:
        last_sends(p, 2)
    for p in parts:
        pass_on(p, 1)
    for p in parts:
        last_sends(p, 3)
    for r in range(2, 4):
        for p in parts:
            pass_on(p, r)
        for p in parts:
            opposite(p, r - 2)
    for r in range(2, 4):
        for p in parts:
            opposite(p, r)
    place_copy.wait()
    slot_copy.wait()
    arrived(twin_slot_ref, er.at[0])
    twin_slot_copy = pltpu.make_async_copy(twin_slot_ref, slot_smem.at[pl.ds(2, 2)], table_sem.at[2])
    twin_slot_copy.start()
    for p in parts:
        arrived(
            gathered.at[pl.ds(BASE[p] + (1 - core) * CHUNKS * UNITS[p], CHUNKS * UNITS[p])], gcr.at[p]
        )

    def block_of(b, slot):
        pieces = [
            gathered[pl.ds(place_smem[0, b, slot], 3)].reshape(3 * UNIT, FIN),
            gathered[pl.ds(place_smem[1, b, slot], 2)].reshape(2 * UNIT, FIN),
            gathered[place_smem[2, b, slot]],
            gathered[pl.ds(place_smem[3, b, slot], 2)].reshape(2 * UNIT, FIN),
        ]
        return jnp.concatenate(pieces, axis=0)

    def forward_step(n, totals):
        new = []
        for b in range(2):
            total = totals[b]
            for k in range(FORWARD_UNROLL):
                slot = (n * FORWARD_UNROLL + k) * 2
                left = jnp.concatenate([tiles[b, slot], tiles[b, slot + 1]], axis=1)
                right = jnp.concatenate([block_of(b, slot), block_of(b, slot + 1)], axis=0)
                total = total + jnp.dot(left, right, preferred_element_type=F32)
            new.append(total)
        return tuple(new)

    zero = jnp.zeros((TILE, FIN), F32)
    totals = lax.fori_loop(0, SLOTS // (2 * FORWARD_UNROLL), forward_step, (zero, zero))
    aggregated = jnp.concatenate(totals, axis=0).astype(BF16)
    weight = w_ref[...]
    pre = jnp.dot(aggregated, weight, preferred_element_type=F32)
    sigma = jax.nn.sigmoid(pre)
    act_ref[...] = (pre * sigma).astype(BF16)
    delta = (ct_ref[...].astype(F32) * sigma * (1.0 + pre * (1.0 - sigma))).astype(BF16)
    back = lax.dot_general(
        weight, delta, (((1,), (1,)), ((), ())), preferred_element_type=F32
    ).astype(BF16)

    for b in range(2):
        left_factor = back[:, b * TILE : (b + 1) * TILE]
        for group in range(2):
            def term_step(n, carry, b=b, group=group, left_factor=left_factor):
                for k in range(TERM_UNROLL):
                    slot = group * 16 + (n * TERM_UNROLL + k) * 2
                    right = jnp.concatenate([tiles[b, slot], tiles[b, slot + 1]], axis=1)
                    both = jnp.dot(left_factor, right, preferred_element_type=F32).astype(BF16)
                    for which in range(2):
                        for p in parts:
                            terms[p][b * SLOTS + slot + which] = both[
                                STARTS[p] : STARTS[p] + ROWS[p], which * TILE : (which + 1) * TILE
                            ]
                return carry

            lax.fori_loop(0, 8 // TERM_UNROLL, term_step, 0)
            for p in parts:
                first = b * SLOTS + group * 16
                send(
                    terms[p].at[pl.ds(first, 16)], terms[p].at[pl.ds(2 * SLOTS + first, 16)],
                    ts.at[p], tr.at[p], twin,
                )
    weight_terms = lax.dot_general(
        aggregated, delta, (((0,), (0,)), ((), ())), preferred_element_type=F32
    )
    for which in range(2):
        wg_ref[pl.ds(which * FIN, FIN), :] = weight_terms[:, which * TILE : (which + 1) * TILE]
    send(wg_ref, twin_wg_ref, es.at[1], er.at[1], twin)
    twin_slot_copy.wait()
    for p in parts:
        arrived(terms[p].at[pl.ds(2 * SLOTS, 2 * SLOTS)], tr.at[p])
    arrived(twin_wg_ref, er.at[1])

    row = lax.broadcasted_iota(I32, (EXTRA, TILE), 0)

    def weight_rows(p, slow, middle, fast):
        moved = {ORDER[p][0]: slow, ORDER[p][1]: middle, ORDER[p][2]: fast}
        target = ((moved[0] * SIDE + moved[1]) * SIDE + moved[2]) * 2 + core
        rows = []
        for which in range(2):
            place = pl.ds(which * FIN + target, 1)
            rows.append(wg_ref[place, :] + twin_wg_ref[place, :])
        return jnp.where(row == 0, rows[0], jnp.where(row == 1, rows[1], 0.0)).astype(BF16)

    def spread(p, slow, middle, dst, extras):
        values = []
        for fast in range(SIDE):
            halves = []
            for which in range(2):
                entry = ((slow * SIDE + middle) * SIDE + fast) * 2 + which
                found = [terms[p][slot_smem[k, core * 4 + p, entry]] for k in range(4)]
                halves.append((found[0] + found[1]) + (found[2] + found[3]))
            if p == 2:
                halves.append(weight_rows(p, slow, middle, fast))
            value = jnp.concatenate(halves, axis=0)
            if extras:
                value = value.astype(F32)
                for extra, first in extras:
                    if 0 <= fast - first < extra.shape[0]:
                        value = value + extra[fast - first].astype(F32)
                value = value.astype(BF16)
            values.append(value)
        for fast in range(SIDE):
            dst[fast] = values[fast]

    away = (2, 1, 0, 3)

    def middle_at(p, q):
        return (at[ORDER[p][1]] + away[q]) % SIDE

    def own_slab(p, o, q, extras=()):
        slow, middle = (at[ORDER[p][0]] + o) % SIDE, middle_at(p, q)
        ref = own[p].at[pl.ds((slow * SIDE + middle) * SIDE, SIDE)]
        spread(p, slow, middle, ref, extras)
        return ref

    up = [device(ORDER[p][0], 1) for p in parts]
    down = [device(ORDER[p][0], 3) for p in parts]
    def start_pass(p, q):
        ref = own_slab(p, 2, q)
        if q < 2:
            send(ref, pass_up[p].at[q], rs.at[p], par.at[p, q], up[p])
        else:
            send(ref, pass_down[p].at[q - 2], rs.at[p], par.at[p, q], down[p])

    def plain_end(p, q):
        if q < 2:
            send(own_slab(p, 3, q), end[p].at[q, 1], rs.at[p], per.at[p, q], down[p])
        else:
            send(own_slab(p, 1, q), end[p].at[q, 0], rs.at[p], per.at[p, q], up[p])

    def passed_end(p, q):
        if q < 2:
            arrived(pass_up[p].at[q], par.at[p, q])
            ref = own_slab(p, 1, q, ((pass_up[p].at[q], 0),))
            send(ref, end[p].at[q, 0], rs.at[p], per.at[p, q], up[p])
        else:
            arrived(pass_down[p].at[q - 2], par.at[p, q])
            ref = own_slab(p, 3, q, ((pass_down[p].at[q - 2], 0),))
            send(ref, end[p].at[q, 1], rs.at[p], per.at[p, q], down[p])

    def finish_slab(p, q):
        arrived(end[p].at[q], per.at[p, q])
        extras = [(end[p].at[q, 0], 0), (end[p].at[q, 1], 0)]
        above, below = device(ORDER[p][1], 1), device(ORDER[p][1], 3)
        if q == 1:
            arrived(mid_pass[p].at[0], bpr.at[p, 0])
            extras.append((mid_pass[p].at[0], 0))
        if q == 3:
            arrived(mid_pass[p].at[1], bpr.at[p, 1])
            extras.append((mid_pass[p].at[1], 2))
        spread(p, at[ORDER[p][0]], middle_at(p, q), mid[p].at[q], extras)
        if q == 0:
            send(mid[p].at[q, pl.ds(0, 2)], mid_pass[p].at[0], rs.at[p], bpr.at[p, 0], above)
            send(mid[p].at[q, pl.ds(2, 2)], mid_pass[p].at[1], rs.at[p], bpr.at[p, 1], below)
        if q == 1:
            send(mid[p].at[q], mid_in[p].at[0], rs.at[p], br.at[p], above)
        if q == 3:
            send(mid[p].at[q], mid_in[p].at[1], rs.at[p], br.at[p], below)

    early, late = (0, 2), (1, 3)
    for what, slabs in (
        (start_pass, early), (plain_end, early), (start_pass, late), (passed_end, early),
        (plain_end, late), (passed_end, late), (finish_slab, early), (finish_slab, late),
    ):
        for q in slabs:
            for p in parts:
                what(p, q)
    for p in parts:
        arrived(mid_in[p], br.at[p])
        total = mid[p][2].astype(F32) + mid_in[p][0].astype(F32) + mid_in[p][1].astype(F32)
        last[p][...] = total.astype(BF16)
        for q, hop in enumerate((2, 1, 3)):
            place = (at[ORDER[p][2]] + hop) % SIDE
            send(last[p].at[place], last_in[p].at[q], rs.at[p], cr.at[p], device(ORDER[p][2], hop))
    results = []
    for p in parts:
        arrived(last_in[p], cr.at[p])
        total = last[p][at[ORDER[p][2]]].astype(F32)
        for q in range(3):
            total = total + last_in[p][q].astype(F32)
        results.append(total)
    for which in range(2):
        block = jnp.concatenate(
            [results[p][which * ROWS[p] : (which + 1) * ROWS[p]] for p in parts], axis=0
        )
        grad_ref[pl.ds(which * TILE, TILE), :] = block.T
    weight_grad_ref[:, pl.ds(0, TILE)] = results[2][64:65]
    weight_grad_ref[:, pl.ds(TILE, TILE)] = results[2][65:66]
    for p in parts:
        sent(gathered.at[pl.ds(BASE[p], 127 * UNITS[p])], gs.at[p])
        sent(terms[p].at[pl.ds(0, 2 * SLOTS)], ts.at[p])
        sent(own[p].at[pl.ds(0, 63)], rs.at[p])
    sent(twin_slot_out, es.at[0])
    sent(wg_ref, es.at[1])


def hand_over(act_in, grad_in, weight_grad_in, act_ref, grad_ref, weight_grad_ref):
    act_ref[...] = act_in[...]
    grad_ref[...] = grad_in[...]
    weight_grad_ref[...] = weight_grad_in[...]


FORWARD_UNROLL = 8
TERM_UNROLL = 8


def on_device(features, weight, tile_values, tile_cols, tile_counts, cotangent):
    def vmem(*shape, dtype=BF16):
        return pltpu.VMEM(shape, dtype)

    def three(*lead, rows):
        return [vmem(*lead, rows[p], TILE) for p in range(3)]

    dma = pltpu.SemaphoreType.DMA
    in_hbm, in_vmem = pl.BlockSpec(memory_space=pltpu.HBM), pl.BlockSpec(memory_space=pltpu.VMEM)
    scratch = (
        [vmem(129 * 16, UNIT, FIN), vmem(FIN, HID), vmem(2, SLOTS, TILE, TILE), vmem(256, HID)]
        + [vmem(2, SLOTS, dtype=I32)] * 2
        + [pltpu.SMEM((2, SLOTS), I32)] * 2
        + [vmem(4, 2, SLOTS, dtype=I32), pltpu.SMEM((4, 2, SLOTS), I32)]
        + [vmem(2, 8, TILE, dtype=I32)] * 3
        + [pltpu.SMEM((4, 8, TILE), I32)]
        + three(NONE + 1, rows=ROWS)
        + three(CHUNKS, rows=CHUNK)
        + three(2, 4, rows=CHUNK)
        + three(2, 4, rows=CHUNK)
        + three(4, 2, 4, rows=CHUNK)
        + three(4, 4, rows=CHUNK)
        + three(2, 2, rows=CHUNK)
        + three(2, 4, rows=CHUNK)
        + three(4, rows=CHUNK)
        + three(3, rows=CHUNK)
        + [vmem(2 * FIN, TILE, dtype=F32)] * 2
        + [dma((8,)), dma((3,)), dma((3,)), dma((3, 3)), dma((3, 12)), dma((3, 8)), dma((3, 4)), dma((3,))]
        + [dma((3,)), dma((3,)), dma((2,)), dma((2,)), dma((3,)), dma((3, 4)), dma((3, 4)), dma((3, 2)), dma((3,)), dma((3,))]
    )
    shapes = (
        jax.ShapeDtypeStruct((256, HID), BF16),
        jax.ShapeDtypeStruct((256, FIN), F32),
        jax.ShapeDtypeStruct((1, HID), F32),
    )
    results = pl.pallas_call(
        kernel,
        out_shape=shapes,
        in_specs=[in_hbm] * 6,
        out_specs=(in_vmem,) * 3,
        scratch_shapes=scratch,
        compiler_params=pltpu.CompilerParams(
            collective_id=0, has_side_effects=True, vmem_limit_bytes=48 << 20
        ),
        name="graph_layer",
    )(*(
        pltpu.with_memory_space_constraint(x, pltpu.HBM)
        for x in (features.reshape(16, UNIT, FIN), weight, tile_values, tile_cols, tile_counts, cotangent)
    ))
    return pl.pallas_call(
        hand_over,
        out_shape=shapes,
        in_specs=[in_vmem] * 3,
        out_specs=(in_vmem,) * 3,
        compiler_params=pltpu.CompilerParams(vmem_limit_bytes=4 << 20),
        name="hand_over",
    )(*results)


def solution(mesh):
    return jax.shard_map(
        on_device,
        mesh=mesh,
        in_specs=(
            P("dev", None),
            P(),
            P("dev", None, None, None),
            P("dev", None),
            P("dev", None),
            P("dev", None),
        ),
        out_specs=(P("dev", None), P("dev", None), P("dev", None)),
        check_vma=False,
    )
```

```python
import jax
import jax.numpy as jnp
from jax import lax
from jax.experimental import pallas as pl
from jax.experimental.pallas import tpu as pltpu
from jax.sharding import PartitionSpec as P

MESH = pl.DeviceIdType.MESH
BF16, F32, I32 = jnp.bfloat16, jnp.float32, jnp.int32
SIDE = 4
TILE, SLOTS, FIN, HID = 128, 32, 128, 256
CHUNKS = 64
UNIT = 16
UNITS = (6, 5, 5)
BASE = (0, 129 * 6, 129 * 11)
ROWS = (48, 48, 32)
STARTS = (0, 48, 96)
EXTRA = 16
CHUNK = (96, 96, 80)
NONE = 4 * SLOTS
ORDER = ((0, 1, 2), (1, 2, 0), (2, 0, 1))
HOPS = (1, 3, 2)


def pick(which, values):
    return jnp.where(which == 0, values[0], jnp.where(which == 1, values[1], values[2]))


def kernel(
    features_hbm, weight_hbm, tiles_hbm, cols_hbm, counts_hbm, cotangent_hbm,
    act_ref, grad_ref, weight_grad_ref,
    gathered, w_ref, tiles, ct_ref, cols_ref, counts_ref, cols_smem, counts_smem,
    place_ref, place_smem, slot_ref, twin_slot_out, twin_slot_ref, slot_smem, t0, t1, t2, own0, own1, own2,
    pass_up0, pass_up1, pass_up2, pass_down0, pass_down1, pass_down2,
    end0, end1, end2,
    b0, b1, b2, bp0, bp1, bp2, rb0, rb1, rb2, c0, c1, c2, rc0, rc1, rc2, wg_ref, twin_wg_ref,
    load_sem, table_sem, gs, g1r, g2r, g3r, gfr, gcr, ts, tr, es, er, rs, par, per, bpr, br, cr,
):
    parts = range(3)
    terms, own = (t0, t1, t2), (own0, own1, own2)
    pass_up, pass_down = (pass_up0, pass_up1, pass_up2), (pass_down0, pass_down1, pass_down2)
    end = (end0, end1, end2)
    mid, mid_pass, mid_in = (b0, b1, b2), (bp0, bp1, bp2), (rb0, rb1, rb2)
    last, last_in = (c0, c1, c2), (rc0, rc1, rc2)

    me = lax.axis_index("dev")
    core = me % 2
    at = (me // 32, (me // 8) % 4, (me // 2) % 4)
    strides = (32, 8, 2)

    def device(axis, hop):
        return (me + ((at[axis] + hop) % SIDE - at[axis]) * strides[axis],)

    twin = (me + 1 - 2 * core,)

    barrier = pltpu.get_barrier_semaphore()
    for hop in (2, 1, 3):
        for axis in range(3):
            pl.semaphore_signal(barrier, inc=1, device_id=device(axis, hop), device_id_type=MESH)
    pl.semaphore_signal(barrier, inc=1, device_id=twin, device_id_type=MESH)

    turn = [(core + p) % 3 for p in parts]
    i3, i2, i1 = ([pick((turn[p] + n) % 3, at) for p in parts] for n in range(3))
    s3, s2, s1 = ([pick((turn[p] + n) % 3, strides) for p in parts] for n in range(3))

    def move(index, stride, hop):
        return (me + ((index + hop) % SIDE - index) * stride,)

    def chunk(p, slow, fast, middle, count=1):
        at_chunk = core * CHUNKS + (slow * SIDE + fast) * SIDE + middle
        return gathered.at[pl.ds(BASE[p] + at_chunk * UNITS[p], count * UNITS[p])]

    loads = []

    def load(src, dst, n):
        copy = pltpu.make_async_copy(src, dst, load_sem.at[n])
        copy.start()
        loads.append(copy)

    for p, first, unit, count in ((0, 0, 0, 3), (1, 3, 0, 3), (2, 6, 0, 2), (0, 8, 3, 3), (1, 11, 3, 2), (2, 13, 2, 3)):
        place = BASE[p] + (core * CHUNKS + (i3[p] * SIDE + i1[p]) * SIDE + i2[p]) * UNITS[p] + unit
        load(features_hbm.at[pl.ds(first, count)], gathered.at[pl.ds(place, count)], 0)
    load(cols_hbm, cols_smem, 1)
    load(counts_hbm, counts_smem, 2)
    load(cols_hbm, cols_ref, 3)
    load(counts_hbm, counts_ref, 4)
    load(tiles_hbm, tiles, 5)
    load(weight_hbm, w_ref, 6)
    load(cotangent_hbm, ct_ref, 7)

    def send(src, dst, ssem, rsem, to):
        copy = pltpu.make_async_remote_copy(
            src_ref=src, dst_ref=dst, send_sem=ssem, recv_sem=rsem, device_id=to, device_id_type=MESH
        )
        copy.start()

    def arrived(dst, rsem):
        pltpu.make_async_remote_copy(
            src_ref=dst, dst_ref=dst, send_sem=es.at[0], recv_sem=rsem, device_id=twin, device_id_type=MESH
        ).wait_recv()

    def sent(src, ssem):
        pltpu.make_async_remote_copy(
            src_ref=src, dst_ref=src, send_sem=ssem, recv_sem=er.at[0], device_id=twin, device_id_type=MESH
        ).wait_send()

    pltpu.make_async_copy(features_hbm, gathered.at[pl.ds(0, 16)], load_sem.at[0]).wait()
    pl.semaphore_wait(barrier, 10)

    def fast_at(p, r):
        return i1[p] if r == 0 else (i1[p] + SIDE - HOPS[r - 1]) % SIDE

    def along_third(p, r, ref):
        for n, hop in enumerate((1, 3)):
            send(ref, ref, gs.at[p], g3r.at[p, 2 * r + n], move(i3[p], s3[p], hop))

    def first_sends(p, r):
        ref = chunk(p, i3[p], fast_at(p, r), i2[p])
        if r > 0:
            arrived(ref, g1r.at[p, r - 1])
        for n, hop in enumerate(HOPS):
            send(ref, ref, gs.at[p], g2r.at[p, r], move(i2[p], s2[p], hop))
        return ref

    for p in parts:
        mine = chunk(p, i3[p], i1[p], i2[p])
        for n, hop in enumerate(HOPS):
            send(mine, mine, gs.at[p], g1r.at[p, n], move(i1[p], s1[p], hop))
    for r in range(4):
        refs = [first_sends(p, r) for p in parts]
        for p in parts:
            along_third(p, r, refs[p])

    def group(p, slow, r, first=0, count=SIDE):
        return chunk(p, slow, fast_at(p, r), first, count)

    def to_the_twin(p, ref):
        send(ref, ref, gs.at[p], gcr.at[p], twin)

    def last_sends(p, r):
        arrived(group(p, i3[p], r, 0, 3), g2r.at[p, r])
        for hop in HOPS:
            along_third(p, r, chunk(p, i3[p], fast_at(p, r), (i2[p] + SIDE - hop) % SIDE))
        to_the_twin(p, group(p, i3[p], r))

    def pass_on(p, r):
        below, above = (i3[p] + 3) % SIDE, (i3[p] + 1) % SIDE
        arrived(group(p, below, r), g3r.at[p, 2 * r])
        half = group(p, below, r, 0, 2)
        send(half, half, gs.at[p], gfr.at[p, r], move(i3[p], s3[p], 1))
        arrived(group(p, above, r), g3r.at[p, 2 * r + 1])
        half = group(p, above, r, 2, 2)
        send(half, half, gs.at[p], gfr.at[p, r], move(i3[p], s3[p], 3))
        to_the_twin(p, group(p, below, r))
        to_the_twin(p, group(p, above, r))

    def opposite(p, r):
        ref = group(p, (i3[p] + 2) % SIDE, r)
        arrived(ref, gfr.at[p, r])
        to_the_twin(p, ref)

    for p in parts:
        last_sends(p, 0)
    for p in parts:
        gathered[pl.ds(BASE[p] + 2 * CHUNKS * UNITS[p], UNITS[p])] = jnp.zeros((UNITS[p], UNIT, FIN), BF16)
        terms[p][NONE] = jnp.zeros((ROWS[p], TILE), BF16)
    for copy in loads[6:]:
        copy.wait()
    cols = cols_ref[...]
    live = counts_ref[...] > 0
    where = (cols >> 6, (cols >> 4) & 3, (cols >> 2) & 3)
    col_core, half = (cols >> 1) & 1, jnp.where(live, cols & 1, 0)
    starts = []
    for p in parts:
        turned = (col_core + p) % 3
        flat = col_core
        for n in (0, 2, 1):
            flat = flat * SIDE + pick((turned + n) % 3, where)
        starts.append(BASE[p] + jnp.where(live, flat, 2 * CHUNKS) * UNITS[p])
    place_ref[0] = starts[0] + 3 * half
    place_ref[1] = starts[1] + 3 * half
    place_ref[2] = jnp.where(half == 0, starts[1], starts[2]) + 2
    place_ref[3] = starts[2] + 3 * half
    place_copy = pltpu.make_async_copy(place_ref, place_smem, table_sem.at[0])
    place_copy.start()
    line = lax.broadcasted_iota(I32, (8, TILE), 0)
    lane = lax.broadcasted_iota(I32, (8, TILE), 1)
    digits = (lane >> 5, (lane >> 3) & 3, (lane >> 1) & 3)
    column = 0
    for axis in range(3):
        digit = pick(line & 3, [digits[ORDER[p].index(axis)] for p in parts])
        column = column * SIDE + digit
    column = column * 4 + (line >> 2) * 2 + (lane & 1)
    for b in range(2):
        def find(s, found, b=b):
            wanted = jnp.where(counts_smem[b, s] > 0, cols_smem[b, s], -1)
            return jnp.where(column == wanted, b * SLOTS + s, found)

        found = lax.fori_loop(0, SLOTS, find, jnp.full((8, TILE), NONE, I32))
        slot_ref[b] = found
        twin_slot_out[b] = jnp.where(found < NONE, found + 2 * SLOTS, NONE)
    send(twin_slot_out, twin_slot_ref, es.at[0], er.at[0], twin)
    slot_copy = pltpu.make_async_copy(slot_ref, slot_smem.at[pl.ds(0, 2)], table_sem.at[1])
    slot_copy.start()
    for p in parts:
        last_sends(p, 1)
    for p in parts:
        pass_on(p, 0)
    for p in parts:
        last_sends(p, 2)
    for p in parts:
        pass_on(p, 1)
    for p in parts:
        last_sends(p, 3)
    for r in range(2, 4):
        for p in parts:
            pass_on(p, r)
        for p in parts:
            opposite(p, r - 2)
    for r in range(2, 4):
        for p in parts:
            opposite(p, r)
    place_copy.wait()
    slot_copy.wait()
    arrived(twin_slot_ref, er.at[0])
    twin_slot_copy = pltpu.make_async_copy(twin_slot_ref, slot_smem.at[pl.ds(2, 2)], table_sem.at[2])
    twin_slot_copy.start()
    for p in parts:
        arrived(
            gathered.at[pl.ds(BASE[p] + (1 - core) * CHUNKS * UNITS[p], CHUNKS * UNITS[p])], gcr.at[p]
        )

    def block_of(b, slot):
        pieces = [
            gathered[pl.ds(place_smem[0, b, slot], 3)].reshape(3 * UNIT, FIN),
            gathered[pl.ds(place_smem[1, b, slot], 2)].reshape(2 * UNIT, FIN),
            gathered[place_smem[2, b, slot]],
            gathered[pl.ds(place_smem[3, b, slot], 2)].reshape(2 * UNIT, FIN),
        ]
        return jnp.concatenate(pieces, axis=0)

    def forward_step(n, totals):
        new = []
        for b in range(2):
            total = totals[b]
            for k in range(FORWARD_UNROLL):
                slot = (n * FORWARD_UNROLL + k) * 2
                left = jnp.concatenate([tiles[b, slot], tiles[b, slot + 1]], axis=1)
                right = jnp.concatenate([block_of(b, slot), block_of(b, slot + 1)], axis=0)
                total = total + jnp.dot(left, right, preferred_element_type=F32)
            new.append(total)
        return tuple(new)

    zero = jnp.zeros((TILE, FIN), F32)
    totals = lax.fori_loop(0, SLOTS // (2 * FORWARD_UNROLL), forward_step, (zero, zero))
    aggregated = jnp.concatenate(totals, axis=0).astype(BF16)
    weight = w_ref[...]
    pre = jnp.dot(aggregated, weight, preferred_element_type=F32)
    sigma = jax.nn.sigmoid(pre)
    act_ref[...] = (pre * sigma).astype(BF16)
    delta = (ct_ref[...].astype(F32) * sigma * (1.0 + pre * (1.0 - sigma))).astype(BF16)
    back = lax.dot_general(
        weight, delta, (((1,), (1,)), ((), ())), preferred_element_type=F32
    ).astype(BF16)

    weight_terms = lax.dot_general(
        aggregated, delta, (((0,), (0,)), ((), ())), preferred_element_type=F32
    )
    for which in range(2):
        wg_ref[pl.ds(which * FIN, FIN), :] = weight_terms[:, which * TILE : (which + 1) * TILE]
    send(wg_ref, twin_wg_ref, es.at[1], er.at[1], twin)

    for b in range(2):
        left_factor = back[:, b * TILE : (b + 1) * TILE]
        for group in range(4):
            def term_step(n, carry, b=b, group=group, left_factor=left_factor):
                for k in range(TERM_UNROLL):
                    slot = group * 8 + (n * TERM_UNROLL + k) * 2
                    right = jnp.concatenate([tiles[b, slot], tiles[b, slot + 1]], axis=1)
                    both = jnp.dot(left_factor, right, preferred_element_type=F32).astype(BF16)
                    for which in range(2):
                        for p in parts:
                            terms[p][b * SLOTS + slot + which] = both[
                                STARTS[p] : STARTS[p] + ROWS[p], which * TILE : (which + 1) * TILE
                            ]
                return carry

            lax.fori_loop(0, 4 // TERM_UNROLL, term_step, 0)
            for p in parts:
                first = b * SLOTS + group * 8
                send(
                    terms[p].at[pl.ds(first, 8)], terms[p].at[pl.ds(2 * SLOTS + first, 8)],
                    ts.at[p], tr.at[p], twin,
                )
    twin_slot_copy.wait()
    for p in parts:
        arrived(terms[p].at[pl.ds(2 * SLOTS, 2 * SLOTS)], tr.at[p])
    arrived(twin_wg_ref, er.at[1])

    row = lax.broadcasted_iota(I32, (EXTRA, TILE), 0)

    def weight_rows(p, slow, middle, fast):
        moved = {ORDER[p][0]: slow, ORDER[p][1]: middle, ORDER[p][2]: fast}
        target = ((moved[0] * SIDE + moved[1]) * SIDE + moved[2]) * 2 + core
        rows = []
        for which in range(2):
            place = pl.ds(which * FIN + target, 1)
            rows.append(wg_ref[place, :] + twin_wg_ref[place, :])
        return jnp.where(row == 0, rows[0], jnp.where(row == 1, rows[1], 0.0)).astype(BF16)

    def spread(p, slow, middle, dst, extras):
        values = []
        for fast in range(SIDE):
            halves = []
            for which in range(2):
                entry = ((slow * SIDE + middle) * SIDE + fast) * 2 + which
                found = [terms[p][slot_smem[k, core * 4 + p, entry]] for k in range(4)]
                halves.append((found[0] + found[1]) + (found[2] + found[3]))
            if p == 2:
                halves.append(weight_rows(p, slow, middle, fast))
            value = jnp.concatenate(halves, axis=0)
            if extras:
                value = value.astype(F32)
                for extra, first in extras:
                    if 0 <= fast - first < extra.shape[0]:
                        value = value + extra[fast - first].astype(F32)
                value = value.astype(BF16)
            values.append(value)
        for fast in range(SIDE):
            dst[fast] = values[fast]

    away = (2, 1, 0, 3)

    def middle_at(p, q):
        return (at[ORDER[p][1]] + away[q]) % SIDE

    def own_slab(p, o, q, extras=()):
        slow, middle = (at[ORDER[p][0]] + o) % SIDE, middle_at(p, q)
        ref = own[p].at[pl.ds((slow * SIDE + middle) * SIDE, SIDE)]
        spread(p, slow, middle, ref, extras)
        return ref

    up = [device(ORDER[p][0], 1) for p in parts]
    down = [device(ORDER[p][0], 3) for p in parts]
    def start_pass(p, q):
        ref = own_slab(p, 2, q)
        if q < 2:
            send(ref, pass_up[p].at[q], rs.at[p], par.at[p, q], up[p])
        else:
            send(ref, pass_down[p].at[q - 2], rs.at[p], par.at[p, q], down[p])

    def plain_end(p, q):
        if q < 2:
            send(own_slab(p, 3, q), end[p].at[q, 1], rs.at[p], per.at[p, q], down[p])
        else:
            send(own_slab(p, 1, q), end[p].at[q, 0], rs.at[p], per.at[p, q], up[p])

    def passed_end(p, q):
        if q < 2:
            arrived(pass_up[p].at[q], par.at[p, q])
            ref = own_slab(p, 1, q, ((pass_up[p].at[q], 0),))
            send(ref, end[p].at[q, 0], rs.at[p], per.at[p, q], up[p])
        else:
            arrived(pass_down[p].at[q - 2], par.at[p, q])
            ref = own_slab(p, 3, q, ((pass_down[p].at[q - 2], 0),))
            send(ref, end[p].at[q, 1], rs.at[p], per.at[p, q], down[p])

    def finish_slab(p, q):
        arrived(end[p].at[q], per.at[p, q])
        extras = [(end[p].at[q, 0], 0), (end[p].at[q, 1], 0)]
        above, below = device(ORDER[p][1], 1), device(ORDER[p][1], 3)
        if q == 1:
            arrived(mid_pass[p].at[0], bpr.at[p, 0])
            extras.append((mid_pass[p].at[0], 0))
        if q == 3:
            arrived(mid_pass[p].at[1], bpr.at[p, 1])
            extras.append((mid_pass[p].at[1], 2))
        spread(p, at[ORDER[p][0]], middle_at(p, q), mid[p].at[q], extras)
        if q == 0:
            send(mid[p].at[q, pl.ds(0, 2)], mid_pass[p].at[0], rs.at[p], bpr.at[p, 0], above)
            send(mid[p].at[q, pl.ds(2, 2)], mid_pass[p].at[1], rs.at[p], bpr.at[p, 1], below)
        if q == 1:
            send(mid[p].at[q], mid_in[p].at[0], rs.at[p], br.at[p], above)
        if q == 3:
            send(mid[p].at[q], mid_in[p].at[1], rs.at[p], br.at[p], below)

    early, late = (0, 2), (1, 3)
    for what, slabs in (
        (start_pass, early), (plain_end, early), (start_pass, late), (passed_end, early),
        (plain_end, late), (passed_end, late), (finish_slab, early), (finish_slab, late),
    ):
        for q in slabs:
            for p in parts:
                what(p, q)
    for p in parts:
        arrived(mid_in[p], br.at[p])
        total = mid[p][2].astype(F32) + mid_in[p][0].astype(F32) + mid_in[p][1].astype(F32)
        last[p][...] = total.astype(BF16)
        for q, hop in enumerate((2, 1, 3)):
            place = (at[ORDER[p][2]] + hop) % SIDE
            send(last[p].at[place], last_in[p].at[q], rs.at[p], cr.at[p], device(ORDER[p][2], hop))
    results = []
    for p in parts:
        arrived(last_in[p], cr.at[p])
        total = last[p][at[ORDER[p][2]]].astype(F32)
        for q in range(3):
            total = total + last_in[p][q].astype(F32)
        results.append(total)
    for which in range(2):
        block = jnp.concatenate(
            [results[p][which * ROWS[p] : (which + 1) * ROWS[p]] for p in parts], axis=0
        )
        grad_ref[pl.ds(which * TILE, TILE), :] = block.T
    weight_grad_ref[:, pl.ds(0, TILE)] = results[2][64:65]
    weight_grad_ref[:, pl.ds(TILE, TILE)] = results[2][65:66]
    for p in parts:
        sent(gathered.at[pl.ds(BASE[p], 127 * UNITS[p])], gs.at[p])
        sent(terms[p].at[pl.ds(0, 2 * SLOTS)], ts.at[p])
        sent(own[p].at[pl.ds(0, 63)], rs.at[p])
    sent(twin_slot_out, es.at[0])
    sent(wg_ref, es.at[1])


def hand_over(act_in, grad_in, weight_grad_in, act_ref, grad_ref, weight_grad_ref):
    act_ref[...] = act_in[...]
    grad_ref[...] = grad_in[...]
    weight_grad_ref[...] = weight_grad_in[...]


FORWARD_UNROLL = 8
TERM_UNROLL = 4


def on_device(features, weight, tile_values, tile_cols, tile_counts, cotangent):
    def vmem(*shape, dtype=BF16):
        return pltpu.VMEM(shape, dtype)

    def three(*lead, rows):
        return [vmem(*lead, rows[p], TILE) for p in range(3)]

    dma = pltpu.SemaphoreType.DMA
    in_hbm, in_vmem = pl.BlockSpec(memory_space=pltpu.HBM), pl.BlockSpec(memory_space=pltpu.VMEM)
    scratch = (
        [vmem(129 * 16, UNIT, FIN), vmem(FIN, HID), vmem(2, SLOTS, TILE, TILE), vmem(256, HID)]
        + [vmem(2, SLOTS, dtype=I32)] * 2
        + [pltpu.SMEM((2, SLOTS), I32)] * 2
        + [vmem(4, 2, SLOTS, dtype=I32), pltpu.SMEM((4, 2, SLOTS), I32)]
        + [vmem(2, 8, TILE, dtype=I32)] * 3
        + [pltpu.SMEM((4, 8, TILE), I32)]
        + three(NONE + 1, rows=ROWS)
        + three(CHUNKS, rows=CHUNK)
        + three(2, 4, rows=CHUNK)
        + three(2, 4, rows=CHUNK)
        + three(4, 2, 4, rows=CHUNK)
        + three(4, 4, rows=CHUNK)
        + three(2, 2, rows=CHUNK)
        + three(2, 4, rows=CHUNK)
        + three(4, rows=CHUNK)
        + three(3, rows=CHUNK)
        + [vmem(2 * FIN, TILE, dtype=F32)] * 2
        + [dma((8,)), dma((3,)), dma((3,)), dma((3, 3)), dma((3, 4)), dma((3, 8)), dma((3, 4)), dma((3,))]
        + [dma((3,)), dma((3,)), dma((2,)), dma((2,)), dma((3,)), dma((3, 4)), dma((3, 4)), dma((3, 2)), dma((3,)), dma((3,))]
    )
    shapes = (
        jax.ShapeDtypeStruct((256, HID), BF16),
        jax.ShapeDtypeStruct((256, FIN), F32),
        jax.ShapeDtypeStruct((1, HID), F32),
    )
    results = pl.pallas_call(
        kernel,
        out_shape=shapes,
        in_specs=[in_hbm] * 6,
        out_specs=(in_vmem,) * 3,
        scratch_shapes=scratch,
        compiler_params=pltpu.CompilerParams(
            collective_id=0, has_side_effects=True, vmem_limit_bytes=48 << 20
        ),
        name="graph_layer",
    )(*(
        pltpu.with_memory_space_constraint(x, pltpu.HBM)
        for x in (features.reshape(16, UNIT, FIN), weight, tile_values, tile_cols, tile_counts, cotangent)
    ))
    return pl.pallas_call(
        hand_over,
        out_shape=shapes,
        in_specs=[in_vmem] * 3,
        out_specs=(in_vmem,) * 3,
        compiler_params=pltpu.CompilerParams(vmem_limit_bytes=4 << 20),
        name="hand_over",
    )(*results)


def solution(mesh):
    return jax.shard_map(
        on_device,
        mesh=mesh,
        in_specs=(
            P("dev", None),
            P(),
            P("dev", None, None, None),
            P("dev", None),
            P("dev", None),
            P("dev", None),
        ),
        out_specs=(P("dev", None), P("dev", None), P("dev", None)),
        check_vma=False,
    )
```
